128 devices in a mesh: dp: 4 (over x), expert: 32 (over y, z, core).
Axes of the slice: x: 4, y: 4, z: 4, core: 2. Of those that a mesh axis runs over, the one named last changes fastest.
Arguments:
- tokens: bfloat16 [16384, 2048], P(('dp', 'expert')), may hold values from -6 to 6
- grad_out: bfloat16 [16384, 2048], P(('dp', 'expert')), may hold values from -6 to 6
- norm_gain: float32 [2048], replicated, may hold values from 0.5 to 1.5
- router: bfloat16 [2048, 32], replicated, may hold values from -0.125 to 0.125
- w_in0: bfloat16 [32, 2048, 2560], P('expert', None, 'dp'), may hold values from -0.125 to 0.125
- w_in1: bfloat16 [32, 2048, 2560], P('expert', None, 'dp'), may hold values from -0.125 to 0.125
- w_out: bfloat16 [32, 2560, 2048], P('expert', 'dp'), may hold values from -0.125 to 0.125
- slot_rows: int32 [128, 32, 8], P(('dp', 'expert')), may hold values from 0 to 127, as said below
- slot_count: int32 [128, 32], P(('dp', 'expert')), may hold values from 0 to 8, as said below
Outputs:
- d_tokens: bfloat16 [16384, 2048], P(('dp', 'expert'))
- d_gain: float32 [2048], replicated
- d_router: float32 [2048, 32], replicated
- d_w_in0: bfloat16 [32, 2048, 2560], P('expert', None, 'dp')
- d_w_in1: bfloat16 [32, 2048, 2560], P('expert', None, 'dp')
- d_w_out: bfloat16 [32, 2560, 2048], P('expert', 'dp')
The draws below stay inside these ranges and needn't reach their ends.
Inputs may be any that keep to these rules, and one draw needn't show every extreme that they name: `slot_rows`: for each sender and expert the 8 entries are distinct rows of that sender. Only the first slot_count slots of a block are live; in every routing group each expert's counts over the group's senders sum to exactly 128, and for every expert and group some sender has all 8 slots live and some sender none.
All inputs are finite; a program needn't handle non-finite values.
Results may differ from the reference program's by a relative error of at most 0.0079.
Values may be sent and summed in bfloat16 or wider, within the bound.
No kernel may reach another device: no remote copies, remote signals or barrier semaphores. Data moves between devices by JAX's collectives and lax.ppermute only.
A program may use at most 128 MiB of HBM per device.

```python
import jax
import jax.numpy as jnp
from jax import lax

D = 2048
FF = 2560
TOK_DEV = 128
SLOTS = 8
EXPERTS = 32
SENDERS = 128
TOKENS = 16384
N_DP = 4
N_EXPERT = 32


def draw_slot_rows(key, part):
    key = jax.random.fold_in(key, 11)
    keys = jax.random.split(key, SENDERS * EXPERTS)

    def first_rows(single):
        return jax.random.permutation(single, TOK_DEV)[:SLOTS]
    orders = jax.vmap(first_rows)(keys)
    return orders.reshape(SENDERS, EXPERTS, SLOTS).astype(jnp.int32)


def draw_slot_count(key, part):
    key = jax.random.fold_in(key, 23)
    keys = jax.random.split(key, N_DP * EXPERTS)
    half = SLOTS // 2

    def group_counts(single):
        order_key, shift_key = jax.random.split(single)
        order = jax.random.permutation(order_key, N_EXPERT).astype(jnp.int32)
        shifts = jax.random.randint(shift_key, (N_EXPERT // 2,), -half, half + 1)
        shifts = shifts.at[0].set(half)
        values = jnp.stack([half + shifts, half - shifts], axis=1).reshape(N_EXPERT)
        return jnp.zeros((N_EXPERT,), jnp.int32).at[order].set(values.astype(jnp.int32))
    counts = jax.vmap(group_counts)(keys).reshape(N_DP, EXPERTS, N_EXPERT)
    counts = jnp.transpose(counts, (0, 2, 1))
    return counts.reshape(SENDERS, EXPERTS).astype(jnp.int32)


def steps_of(key, dims, shards, smallest, largest):
    level = 1.0
    for axis_at, parts in shards:
        heights = jax.random.uniform(jax.random.fold_in(jax.random.fold_in(key, 6), axis_at), (parts,), jnp.float32, smallest / len(shards), largest / len(shards))
        level = level * jnp.repeat(jnp.exp(heights), dims[axis_at] // parts).reshape((-1,) + (1,) * (len(dims) - 1 - axis_at))
    return level


def centred(stream_key, shape, width, bound, shards=(), kind=jnp.bfloat16):
    values = width * jax.random.normal(stream_key, shape, jnp.float32)
    if shards:
        values = values * steps_of(stream_key, shape, shards, -0.22, 0.18)
    return jnp.clip(values, -bound, bound).astype(kind)


def setup_inputs(seed: int = 0) -> dict:
    key_list = jax.random.split(jax.random.key(seed), 10)
    tokens = centred(key_list[0], (TOKENS, D), 1.0, 6.0, ((0, 128),))
    grad_out = centred(key_list[1], (TOKENS, D), 1.0, 6.0, ((0, 128),))
    norm_gain = jnp.clip(1.0 + 0.1 * jax.random.normal(key_list[2], (D,), jnp.float32), 0.5, 1.5)
    router = centred(key_list[3], (D, EXPERTS), D ** -0.5, 0.125)
    w_in0 = centred(key_list[4], (EXPERTS, D, FF), D ** -0.5, 0.125, ((0, 32), (2, 4)))
    w_in1 = centred(key_list[5], (EXPERTS, D, FF), D ** -0.5, 0.125, ((0, 32), (2, 4)))
    w_out = centred(key_list[6], (EXPERTS, FF, D), FF ** -0.5, 0.125, ((0, 32), (1, 4)))
    slot_rows = draw_slot_rows(jax.random.fold_in(key_list[9], 71), 0)
    slot_count = draw_slot_count(jax.random.fold_in(key_list[9], 71), 0)
    return dict(tokens=tokens, grad_out=grad_out, norm_gain=norm_gain, router=router, w_in0=w_in0, w_in1=w_in1, w_out=w_out, slot_rows=slot_rows, slot_count=slot_count)


def gelu_parts(pre):

    def gelu_tanh(value):
        return jax.nn.gelu(value, approximate=True)
    return jax.vjp(gelu_tanh, pre)

def reference(tokens, grad_out, norm_gain, router, w_in0, w_in1, w_out, slot_rows, slot_count):
    highest = lax.Precision.HIGHEST
    tok_float = tokens.astype(jnp.float32)
    inv_rms = lax.rsqrt(lax.optimization_barrier(jnp.mean(tok_float * tok_float, axis=-1, keepdims=True)) + 1e-06)
    normed = (tok_float * inv_rms * norm_gain).astype(jnp.bfloat16)
    gate = jax.nn.sigmoid(jnp.dot(normed, router, preferred_element_type=jnp.float32))
    normed3 = normed.reshape(SENDERS, TOK_DEV, D)
    grad3 = grad_out.reshape(SENDERS, TOK_DEV, D)
    gate3 = gate.reshape(SENDERS, TOK_DEV, EXPERTS)
    sender_ids = jnp.arange(SENDERS, dtype=jnp.int32)[:, None]
    slot_ids = jnp.arange(SLOTS, dtype=jnp.int32)[None, :]

    def per_expert(carry, inputs):
        dh_total, dgate_total = carry
        weight0, weight1, weight_out, rows, count, expert = inputs
        live = slot_ids < count[:, None]
        live_rows = live.astype(jnp.bfloat16)[..., None]
        in_rows = (normed3[sender_ids, rows] * live_rows).reshape(-1, D)
        dy_rows = (grad3[sender_ids, rows] * live_rows).reshape(-1, D)
        gate_rows = jnp.where(live, gate3[sender_ids, rows, expert], 0.0).astype(jnp.bfloat16).reshape(-1)
        pre0 = jnp.dot(in_rows, weight0, preferred_element_type=jnp.float32)
        pre1 = jnp.dot(in_rows, weight1, preferred_element_type=jnp.float32)
        activated, pullback = gelu_parts(pre0)
        act = (activated * pre1).astype(jnp.bfloat16)
        expert_out = jnp.dot(act, weight_out, preferred_element_type=jnp.float32)
        dgate_rows = lax.optimization_barrier(jnp.sum(dy_rows.astype(jnp.float32) * expert_out, axis=-1))
        dy_gated = (gate_rows.astype(jnp.float32)[:, None] * dy_rows.astype(jnp.float32)).astype(jnp.bfloat16)
        grad_wout = jnp.dot(act.T, dy_gated, preferred_element_type=jnp.float32).astype(jnp.bfloat16)
        d_act = jnp.dot(dy_gated, weight_out.T, preferred_element_type=jnp.float32)
        d_pre1 = (d_act * activated).astype(jnp.bfloat16)
        d_pre0 = pullback(d_act * pre1)[0].astype(jnp.bfloat16)
        grad_w0 = jnp.dot(in_rows.T, d_pre0, preferred_element_type=jnp.float32).astype(jnp.bfloat16)
        grad_w1 = jnp.dot(in_rows.T, d_pre1, preferred_element_type=jnp.float32).astype(jnp.bfloat16)
        dh_rows = jnp.dot(d_pre0, weight0.T, preferred_element_type=jnp.float32) + jnp.dot(d_pre1, weight1.T, preferred_element_type=jnp.float32)
        dh_total = dh_total.at[sender_ids, rows].add(dh_rows.reshape(SENDERS, SLOTS, D))
        dgate_total = dgate_total.at[sender_ids, rows, expert].add(dgate_rows.reshape(SENDERS, SLOTS))
        return ((dh_total, dgate_total), (grad_w0, grad_w1, grad_wout))
    start = (jnp.zeros((SENDERS, TOK_DEV, D), jnp.float32), jnp.zeros((SENDERS, TOK_DEV, EXPERTS), jnp.float32))
    inputs = (w_in0, w_in1, w_out, jnp.transpose(slot_rows, (1, 0, 2)), slot_count.T, jnp.arange(EXPERTS, dtype=jnp.int32))
    (dh_total, dgate_total), (d_w_in0, d_w_in1, d_w_out) = lax.scan(per_expert, start, inputs)
    dgate = dgate_total.reshape(TOKENS, EXPERTS)
    dlogit = dgate * gate * (1.0 - gate)
    d_normed = dh_total.reshape(TOKENS, D) + jnp.dot(dlogit, router.astype(jnp.float32).T, precision=highest)
    d_router = jnp.dot(normed.astype(jnp.float32).T, dlogit, precision=highest)
    d_gain = lax.optimization_barrier(jnp.sum(d_normed * tok_float * inv_rms, axis=0))
    scaled = d_normed * norm_gain
    d_tokens = grad_out.astype(jnp.float32) + inv_rms * scaled - tok_float * inv_rms ** 3 * lax.optimization_barrier(jnp.mean(scaled * tok_float, axis=-1, keepdims=True))
    return (d_tokens.astype(jnp.bfloat16), d_gain, d_router, d_w_in0, d_w_in1, d_w_out)
```

```python
import functools

import jax
import jax.numpy as jnp
from jax import lax
from jax.experimental import pallas as pl
from jax.experimental.pallas import tpu as pltpu
from jax.sharding import PartitionSpec as P

F32 = jnp.float32
BF16 = jnp.bfloat16
DEAD = 2.0**100
GELU_SCALE = 0.7978845608028654
GELU_CUBIC = 0.044715


def dot(a, b, dims=((1,), (0,))):
    return lax.dot_general(a, b, (dims, ((), ())), preferred_element_type=F32)


def block_kernel(
    in_ref, dy_ref, w0_ref, w1_ref, wo_ref, rrow_ref, dh_ref, act_ref, d0_ref, d1_ref, col_ref
):
    rows = in_ref[...]
    pre0 = dot(rows, w0_ref[...])
    pre1 = dot(rows, w1_ref[...])
    up = dot(dy_ref[...], wo_ref[...], ((1,), (1,)))
    rows32 = rows.astype(F32)
    rrow = rrow_ref[...]
    logit = jnp.sum(rows32 * rrow, axis=1, keepdims=True)
    gate = 1.0 / (1.0 + jnp.exp(-logit))
    gate_row = gate.astype(BF16).astype(F32)
    square = pre0 * pre0
    tanh = jnp.tanh(GELU_SCALE * pre0 * (1.0 + GELU_CUBIC * square))
    cdf = 0.5 + 0.5 * tanh
    slope = cdf + 0.5 * pre0 * (1.0 - tanh * tanh) * (
        GELU_SCALE * (1.0 + 3.0 * GELU_CUBIC * square)
    )
    gelu = pre0 * cdf
    act = gelu * pre1
    dgate = jnp.sum(act * up, axis=1, keepdims=True)
    d_act = gate_row * up
    d0 = (d_act * pre1 * slope).astype(BF16)
    d1 = (d_act * gelu).astype(BF16)
    act_ref[...] = (gate_row * act).astype(BF16)
    d0_ref[...] = d0
    d1_ref[...] = d1
    dlogit = dgate * gate * (1.0 - gate)
    dh = dot(d0, w0_ref[...], ((1,), (1,))) + dot(d1, w1_ref[...], ((1,), (1,)))
    dh = dh + dlogit * rrow
    dh_ref[...] = dh.astype(dh_ref.dtype)
    col_ref[0:1, :] = jnp.sum(rows32 * dlogit, axis=0, keepdims=True)
    col_ref[1:2, :] = jnp.sum(rows32 * dh, axis=0, keepdims=True)


def block(rows, dy, w0, w1, wo, rrow):
    m, width = rows.shape
    hidden = w0.shape[1]
    whole = pl.BlockSpec(memory_space=pltpu.VMEM)
    return pl.pallas_call(
        block_kernel,
        out_shape=(
            jax.ShapeDtypeStruct((m, width), BF16),
            jax.ShapeDtypeStruct((m, hidden), BF16),
            jax.ShapeDtypeStruct((m, hidden), BF16),
            jax.ShapeDtypeStruct((m, hidden), BF16),
            jax.ShapeDtypeStruct((2, width), F32),
        ),
        in_specs=[whole] * 6,
        out_specs=[whole] * 5,
        compiler_params=pltpu.CompilerParams(vmem_limit_bytes=32 * 1024 * 1024),
        cost_estimate=pl.CostEstimate(
            flops=10 * m * width * hidden, bytes_accessed=6 * width * hidden, transcendentals=0
        ),
        name="block",
    )(rows, dy, w0, w1, wo, rrow)


def shift(value, axis, by):
    n = lax.axis_size(axis)
    return lax.ppermute(value, axis, [(i, (i + by) % n) for i in range(n)])


def exchange(value):
    return lax.all_to_all(value, "expert", split_axis=0, concat_axis=0, tiled=True)


def per_device(tokens, grad_out, norm_gain, router, w_in0, w_in1, w_out, slot_rows, slot_count):
    tok_dev, width = tokens.shape
    experts = router.shape[1]
    slots = slot_rows.shape[2]
    n_dp = lax.axis_size("dp")
    total = experts * slots
    live_rows = total // 2
    w0, w1, wo = w_in0[0], w_in1[0], w_out[0]

    tok_float = tokens.astype(F32)
    inv_rms = lax.rsqrt(jnp.mean(tok_float * tok_float, axis=-1, keepdims=True) + 1e-06)
    normed = (tok_float * inv_rms * norm_gain).astype(BF16)
    live = jnp.arange(slots, dtype=jnp.int32)[None, :] < slot_count[0][:, None]
    named = jnp.where(live, slot_rows[0], -1).reshape(total, 1)
    picker = (named == jnp.arange(tok_dev, dtype=jnp.int32)[None, :]).astype(BF16)
    in_slots = jnp.where(named >= 0, dot(picker, normed), DEAD).astype(BF16)
    dy_slots = dot(picker, grad_out).astype(BF16)
    in_recv = exchange(in_slots.reshape(experts, slots, width)).reshape(total, width)
    dy_recv = exchange(dy_slots.reshape(experts, slots, width)).reshape(total, width)

    alive = (in_recv[:, 0:1] < DEAD / 2).astype(BF16)
    ids = jnp.arange(total, dtype=jnp.int32)
    upto = (ids[:, None] <= ids[None, :]).astype(BF16)
    place = dot(alive, upto, ((0,), (0,)))
    place = jnp.where(alive.reshape(1, total) > 0, place, 0.0)
    wanted = jnp.arange(1, live_rows + 1, dtype=jnp.int32).astype(F32)[:, None]
    compact = (place == wanted).astype(BF16)
    in_own = dot(compact, in_recv).astype(BF16)
    dy_own = dot(compact, dy_recv).astype(BF16)

    expert = lax.axis_index("expert")
    rrow = lax.dynamic_slice_in_dim(router, expert, 1, axis=1).reshape(1, width).astype(F32)

    order = [1, n_dp - 1] + list(range(2, n_dp - 1))
    ins = [in_own] + [shift(in_own, "dp", by) for by in order]
    dys = [dy_own] + [shift(dy_own, "dp", by) for by in order]
    parts = [block(a, b, w0, w1, wo, rrow) for a, b in zip(ins, dys)]

    dh = parts[0][0].astype(F32)
    for by, part in zip(order, parts[1:]):
        dh = dh + shift(part[0], "dp", n_dp - by).astype(F32)
    back = dot(compact, dh.astype(BF16), ((0,), (0,))).astype(BF16)
    back = exchange(back.reshape(experts, slots, width)).reshape(total, width)

    small = sum(part[4] for part in parts)
    small = small + sum(shift(small, "dp", by) for by in order)
    small = exchange(jnp.broadcast_to(small[None], (experts,) + small.shape))
    d_router = small[:, 0, :].T
    d_gain = jnp.sum(small[:, 1, :], axis=0) / norm_gain

    in_all = jnp.concatenate(ins, axis=0)
    dy_all = jnp.concatenate(dys, axis=0)
    act_all, d0_all, d1_all = (jnp.concatenate([p[i] for p in parts], axis=0) for i in (1, 2, 3))
    grad_w0 = dot(in_all, d0_all, ((0,), (0,))).astype(BF16)
    grad_w1 = dot(in_all, d1_all, ((0,), (0,))).astype(BF16)
    grad_wout = dot(act_all, dy_all, ((0,), (0,))).astype(BF16)

    d_normed = dot(picker, back, ((0,), (0,)))
    scaled = d_normed * norm_gain
    d_tokens = (
        grad_out.astype(F32)
        + inv_rms * scaled
        - tok_float * inv_rms**3 * jnp.mean(scaled * tok_float, axis=-1, keepdims=True)
    )
    return (
        d_tokens.astype(BF16),
        d_gain,
        d_router,
        grad_w0[None],
        grad_w1[None],
        grad_wout[None],
    )


def solution(mesh):
    in_specs = (
        P(("dp", "expert"), None),
        P(("dp", "expert"), None),
        P(),
        P(),
        P("expert", None, "dp"),
        P("expert", None, "dp"),
        P("expert", "dp", None),
        P(("dp", "expert"), None, None),
        P(("dp", "expert"), None),
    )
    out_specs = (
        P(("dp", "expert"), None),
        P(),
        P(),
        P("expert", None, "dp"),
        P("expert", None, "dp"),
        P("expert", "dp", None),
    )
    return jax.shard_map(
        per_device, mesh=mesh, in_specs=in_specs, out_specs=out_specs, check_vma=False
    )
```

```python
import functools

import jax
import jax.numpy as jnp
from jax import lax
from jax.experimental import pallas as pl
from jax.experimental.pallas import tpu as pltpu
from jax.sharding import PartitionSpec as P

F32 = jnp.float32
BF16 = jnp.bfloat16
DEAD = 2.0**100
GELU_SCALE = 0.7978845608028654
GELU_CUBIC = 0.044715


def dot(a, b, dims=((1,), (0,))):
    return lax.dot_general(a, b, (dims, ((), ())), preferred_element_type=F32)


WHOLE = pl.BlockSpec(memory_space=pltpu.VMEM)
PARAMS = pltpu.CompilerParams(vmem_limit_bytes=24 * 1024 * 1024)
TAIL = 16
COST = pl.CostEstimate(flops=1, bytes_accessed=1, transcendentals=0)


def stack(refs):
    values = [ref[...] for ref in refs]
    return values[0] if len(values) == 1 else jnp.concatenate(values, axis=0)


def iota(shape, axis):
    return lax.broadcasted_iota(jnp.int32, shape, axis)


def one_hot_of_slots(slot_rows_ref, count_ref, tok_dev, copies):
    slots, experts = slot_rows_ref.shape
    total = copies * slots * experts
    mine = iota((total, experts), 1) == iota((total, experts), 0) // (copies * slots)
    names = dot(
        mine.astype(BF16), slot_rows_ref[...].astype(F32).astype(BF16), ((1,), (1,))
    )
    place = iota((total, slots), 0) % slots
    name = jnp.where(place == iota((total, slots), 1), names, 0.0)
    name = jnp.sum(name, axis=1, keepdims=True)
    count = jnp.where(mine, count_ref[...].astype(F32), 0.0)
    live = place[:, :1].astype(F32) < jnp.sum(count, axis=1, keepdims=True)
    hot = (iota((total, tok_dev), 1).astype(F32) == name) & live
    return hot.astype(BF16), live


def pick_kernel(tokens_ref, grad_ref, gain_ref, slot_rows_ref, count_ref, slots_ref, picker_ref):
    tok_dev = picker_ref.shape[1]
    slots = slot_rows_ref.shape[0]
    picker_ref[...], _ = one_hot_of_slots(slot_rows_ref, count_ref, tok_dev, 1)
    tok = tokens_ref[...].astype(F32)
    inv_rms = lax.rsqrt(jnp.mean(tok * tok, axis=1, keepdims=True) + 1e-06)
    normed = (tok * inv_rms * gain_ref[...]).astype(BF16)
    hot, live = one_hot_of_slots(slot_rows_ref, count_ref, tok_dev, 2)
    second = iota(hot.shape, 0) // slots % 2 == 1
    hot = jnp.concatenate(
        [jnp.where(second, 0.0, hot), jnp.where(second, hot, 0.0)], axis=1
    ).astype(BF16)
    rows = dot(hot, jnp.concatenate([normed, grad_ref[...]], axis=0))
    slots_ref[...] = jnp.where(live, rows, DEAD).astype(BF16)


def pick(tokens, grad_out, norm_gain, slot_rows, slot_count):
    total = slot_rows.shape[0] * slot_rows.shape[1]
    tok_dev, width = tokens.shape
    return pl.pallas_call(
        pick_kernel,
        out_shape=(
            jax.ShapeDtypeStruct((2 * total, width), BF16),
            jax.ShapeDtypeStruct((total, tok_dev), BF16),
        ),
        in_specs=[WHOLE] * 5,
        out_specs=[WHOLE] * 2,
        compiler_params=pltpu.CompilerParams(vmem_limit_bytes=56 * 1024 * 1024),
        cost_estimate=COST,
        name="pick",
    )(tokens, grad_out, norm_gain, slot_rows, slot_count)


def pack_kernel(slots, rows_ref, in_ref, dy_ref, home_ref):
    both = rows_ref.shape[0]
    total, live_rows = home_ref.shape
    rows = rows_ref[...]
    alive = jnp.broadcast_to((rows[:, :1].astype(F32) < DEAD / 2).astype(F32), (both, total))
    second = iota((both, both), 0) // slots % 2
    earlier = (iota((both, both), 1) < iota((both, both), 0)) & (
        iota((both, both), 1) // slots % 2 == second
    )
    index = dot(earlier.astype(BF16), alive.astype(BF16))
    index = index + (live_rows * second[:, :total]).astype(F32)
    wanted = iota((both, total), 1).astype(F32)
    home = ((index == wanted) & (alive > 0.0)).astype(BF16)
    live = dot(home, rows, ((0,), (0,))).astype(BF16)
    in_ref[...] = live[:live_rows]
    dy_ref[...] = live[live_rows:]
    line = iota((total, both), 0)
    source = line // slots * (2 * slots) + line % slots
    first = (iota((total, both), 1) == source).astype(BF16)
    home_ref[...] = dot(first, home[:, :live_rows]).astype(BF16)


def pack(rows, slots):
    both, width = rows.shape
    total = both // 2
    live_rows = total // 2
    return pl.pallas_call(
        functools.partial(pack_kernel, slots),
        out_shape=(
            jax.ShapeDtypeStruct((live_rows, width), BF16),
            jax.ShapeDtypeStruct((live_rows, width), BF16),
            jax.ShapeDtypeStruct((total, live_rows), BF16),
        ),
        in_specs=[WHOLE],
        out_specs=[WHOLE] * 3,
        compiler_params=PARAMS,
        cost_estimate=COST,
        name="pack",
    )(rows)


def hidden_kernel(sizes, *refs):
    pieces = sum(sizes)
    w0_ref, w1_ref = refs[pieces : pieces + 2]
    outs = refs[pieces + 2 :]
    rows = stack(refs[:pieces])
    pre0 = dot(rows, w0_ref[...])
    pre1 = dot(rows, w1_ref[...])
    square = pre0 * pre0
    tanh = jnp.tanh(GELU_SCALE * pre0 * (1.0 + GELU_CUBIC * square))
    cdf = 0.5 + 0.5 * tanh
    slope = cdf + 0.5 * pre0 * (1.0 - tanh * tanh) * (
        GELU_SCALE * (1.0 + 3.0 * GELU_CUBIC * square)
    )
    gelu = pre0 * cdf
    mix = pre1 * slope
    act = gelu * pre1
    start = 0
    for k in range(len(sizes)):
        stop = start + outs[3 * k].shape[0]
        outs[3 * k][...] = gelu[start:stop]
        outs[3 * k + 1][...] = mix[start:stop]
        outs[3 * k + 2][...] = act[start:stop]
        start = stop


def hidden(sets, w0, w1):
    width, units = w0.shape
    sizes = tuple(len(pieces) for pieces in sets)
    rows = [sum(piece.shape[0] for piece in pieces) for pieces in sets]
    flat = pl.pallas_call(
        functools.partial(hidden_kernel, sizes),
        out_shape=[jax.ShapeDtypeStruct((m, units), F32) for m in rows for _ in range(3)],
        in_specs=[WHOLE] * (sum(sizes) + 2),
        out_specs=[WHOLE] * (3 * len(sets)),
        compiler_params=PARAMS,
        cost_estimate=COST,
        name="hidden",
    )(*[piece for pieces in sets for piece in pieces], w0, w1)
    return [flat[3 * k : 3 * k + 3] for k in range(len(sets))]


def block_kernel(n_in, n_dy, outs_n, *refs):
    in_refs, dy_refs, refs = refs[:n_in], refs[n_in : n_in + n_dy], refs[n_in + n_dy :]
    gelu_ref, mix_ref, act_ref, w0_ref, w1_ref, wo_ref, rrow_ref, before_ref = refs[:8]
    outs = refs[8:]
    dh_refs = outs[:outs_n]
    actg_ref, d0_ref, d1_ref, small_ref = outs[outs_n:]
    rrow = rrow_ref[...]
    up = dot(stack(dy_refs), wo_ref[...], ((1,), (1,)))
    rows32 = stack(in_refs).astype(F32)
    logit = jnp.sum(rows32 * rrow, axis=1, keepdims=True)
    gate = 1.0 / (1.0 + jnp.exp(-logit))
    gate_row = gate.astype(BF16).astype(F32)
    act = act_ref[...]
    dgate = jnp.sum(act * up, axis=1, keepdims=True)
    d_act = gate_row * up
    d0 = (d_act * mix_ref[...]).astype(BF16)
    d1 = (d_act * gelu_ref[...]).astype(BF16)
    actg_ref[...] = (gate_row * act).astype(BF16)
    d0_ref[...] = d0
    d1_ref[...] = d1
    dlogit = dgate * gate * (1.0 - gate)
    dh = dot(d0, w0_ref[...], ((1,), (1,))) + dot(d1, w1_ref[...], ((1,), (1,)))
    dh = dh + dlogit * rrow
    col = jnp.sum(rows32 * dlogit, axis=0, keepdims=True)
    gain = jnp.sum(rows32 * dh, axis=0, keepdims=True)
    small = before_ref[...] + jnp.concatenate([col, gain], axis=0)
    small_ref[...] = small
    start = 0
    for ref in dh_refs:
        rows_here = dh.shape[0] // len(dh_refs)
        ref[:rows_here, :] = dh[start : start + rows_here].astype(BF16)
        start += rows_here
        if ref.shape[0] > rows_here:
            high = small.astype(BF16)
            low = (small - high.astype(F32)).astype(BF16)
            rest = jnp.zeros((TAIL - 4, small.shape[1]), BF16)
            ref[rows_here:, :] = jnp.concatenate([high, low, rest], axis=0)


def block(ins, dys, mids, weights, before, outs_n, tail=0):
    w0 = weights[0]
    width, units = w0.shape
    m = sum(piece.shape[0] for piece in ins)
    flat = pl.pallas_call(
        functools.partial(block_kernel, len(ins), len(dys), outs_n),
        out_shape=[jax.ShapeDtypeStruct((m // outs_n + tail, width), BF16)] * outs_n
        + [jax.ShapeDtypeStruct((m, units), BF16)] * 3
        + [jax.ShapeDtypeStruct((2, width), F32)],
        in_specs=[WHOLE] * (len(ins) + len(dys) + 8),
        out_specs=[WHOLE] * (outs_n + 4),
        compiler_params=PARAMS,
        cost_estimate=COST,
        name="block",
    )(*ins, *dys, *mids, *weights, before)
    return flat[:outs_n], flat[outs_n : outs_n + 3], flat[-1]


def expand_kernel(own_ref, after_ref, before_ref, far_ref, home_ref, small_ref, *refs):
    *others, out_ref = refs
    rows, width = own_ref.shape
    dh = sum(ref[...].astype(F32) for ref in (own_ref, after_ref, before_ref))
    dh = dh + far_ref[:rows, :].astype(F32)
    out_ref[:, :width] = dot(home_ref[...], dh.astype(BF16)).astype(BF16)
    carried = far_ref[rows:, :].astype(F32)
    small = small_ref[...] + carried[0:2] + carried[2:4]
    for ref in others:
        small = small + ref[...]
    part = out_ref.shape[1] - width
    lines = [small[k : k + 1, at : at + part] for k in range(2) for at in range(0, width, part)]
    lines = jnp.concatenate(lines, axis=0).astype(BF16)
    out_ref[:, width:] = jnp.concatenate([lines] * (out_ref.shape[0] // lines.shape[0]), axis=0)


def expand(own, after, before, far, home, slots, *smalls):
    total = home.shape[0]
    width = own.shape[1]
    return pl.pallas_call(
        expand_kernel,
        out_shape=jax.ShapeDtypeStruct((total, width + 2 * width // slots), BF16),
        in_specs=[WHOLE] * (5 + len(smalls)),
        out_specs=WHOLE,
        compiler_params=PARAMS,
        cost_estimate=COST,
        name="expand",
    )(own, after, before, far, home, *smalls)


def finish_kernel(
    back_ref, picker_ref, tokens_ref, grad_ref, gain_ref, d_tokens_ref, d_gain_ref, d_router_ref
):
    total = back_ref.shape[0]
    width = tokens_ref.shape[1]
    experts = d_router_ref.shape[0]
    slots = total // experts
    half = slots // 2
    part = back_ref.shape[1] - width
    gain = gain_ref[...]
    tok = tokens_ref[...].astype(F32)
    inv_rms = lax.rsqrt(jnp.mean(tok * tok, axis=1, keepdims=True) + 1e-06)
    d_normed = dot(picker_ref[...], back_ref[:, :width], ((0,), (0,)))
    scaled = d_normed * gain
    inner = jnp.mean(scaled * tok, axis=1, keepdims=True)
    d_tokens_ref[...] = (
        grad_ref[...].astype(F32) + inv_rms * scaled - tok * (inv_rms * inv_rms * inv_rms * inner)
    ).astype(BF16)
    extra = back_ref[:, width:]
    slot = lax.broadcasted_iota(jnp.int32, (experts, total), 1)
    home = slots * lax.broadcasted_iota(jnp.int32, (experts, total), 0)
    place = lax.broadcasted_iota(jnp.int32, (slots, total), 1) % slots
    line = lax.broadcasted_iota(jnp.int32, (slots, total), 0)
    sums = dot((place == line).astype(BF16), extra)
    for q in range(half):
        at = slice(q * part, (q + 1) * part)
        d_router_ref[:, at] = dot((slot == home + q).astype(BF16), extra)
        d_gain_ref[:, at] = sums[half + q : half + q + 1, :] / gain[:, at]


def finish(back, picker, tokens, grad_out, norm_gain, experts):
    width = tokens.shape[1]
    return pl.pallas_call(
        finish_kernel,
        out_shape=(
            jax.ShapeDtypeStruct(tokens.shape, BF16),
            jax.ShapeDtypeStruct((1, width), F32),
            jax.ShapeDtypeStruct((experts, width), F32),
        ),
        in_specs=[WHOLE] * 5,
        out_specs=[WHOLE] * 3,
        compiler_params=PARAMS,
        cost_estimate=COST,
        name="finish",
    )(back, picker, tokens, grad_out, norm_gain)


def in_grads_kernel(n, *refs):
    w0_ref, w1_ref, pair_ref = refs[-3:]
    grads = refs[n:-3]
    units = w0_ref.shape[1]

    @pl.when(pl.program_id(0) == 0)
    def _():
        pair_ref[:, :units] = stack(grads[0::2])
        pair_ref[:, units:] = stack(grads[1::2])

    pair = dot(stack(refs[:n]), pair_ref[...], ((0,), (0,)))
    w0_ref[...] = pair[:, :units].astype(BF16)
    w1_ref[...] = pair[:, units:].astype(BF16)


def out_grad_kernel(n, *refs):
    wo_ref, act_ref = refs[-2:]

    @pl.when(pl.program_id(0) == 0)
    def _():
        act_ref[...] = stack(refs[n:-2]).T

    wo_ref[...] = dot(act_ref[...], stack(refs[:n])).astype(BF16)


def weight_grads(kernel, pieces, factors, outs, scratch, tile=512):
    width = pieces[0].shape[1]
    return pl.pallas_call(
        functools.partial(kernel, len(pieces)),
        grid=(width // tile,),
        out_shape=[jax.ShapeDtypeStruct(shape, BF16) for shape in outs],
        in_specs=[pl.BlockSpec((piece.shape[0], tile), lambda i: (0, i)) for piece in pieces]
        + [pl.BlockSpec(value.shape, lambda i: (0, 0)) for value in factors],
        out_specs=[
            pl.BlockSpec((tile, shape[1]), lambda i: (i, 0))
            if shape[0] == width
            else pl.BlockSpec((shape[0], tile), lambda i: (0, i))
            for shape in outs
        ],
        scratch_shapes=[pltpu.VMEM(scratch, BF16)],
        compiler_params=PARAMS,
        cost_estimate=pl.CostEstimate(flops=1000000000, bytes_accessed=1, transcendentals=0),
        name="weight_grads",
    )(*pieces, *factors)


def shift(value, axis, by):
    n = lax.axis_size(axis)
    return lax.ppermute(value, axis, [(i, (i + by) % n) for i in range(n)])


def exchange(value):
    return lax.all_to_all(value, "expert", split_axis=0, concat_axis=0, tiled=True)


def pass_on(after, before):
    half = after.shape[0] // 2
    return [shift(after[:half], "dp", 1), shift(before[half:], "dp", -1)]


def per_device(tokens, grad_out, norm_gain, router, w_in0, w_in1, w_out, slot_rows, slot_count):
    tok_dev, width = tokens.shape
    experts = router.shape[1]
    slots = slot_rows.shape[2]
    total = experts * slots
    w0, w1, wo = w_in0[0], w_in1[0], w_out[0]

    expert = lax.axis_index("expert")
    rrow = lax.dynamic_slice_in_dim(router.T, expert, 1, axis=0).astype(F32)
    both, picker = pick(
        tokens, grad_out, norm_gain.reshape(1, width), slot_rows[0].T, slot_count
    )
    both = exchange(both.reshape(experts, 2 * slots, width)).reshape(2 * total, width)
    both, rrow = lax.optimization_barrier((both, rrow))
    in_own, dy_own, home = pack(both, slots)
    in_near = [shift(in_own, "dp", by) for by in (1, -1)]
    dy_near = [shift(dy_own, "dp", by) for by in (1, -1)]
    in_far = pass_on(*in_near)
    weights = (w0, w1, wo, rrow)
    mids_own, mids_near = hidden([[in_own], in_near], w0, w1)
    start = jnp.zeros((2, width), F32)
    (dh_own,), grads_own, small = block([in_own], [dy_own], mids_own, weights, start, 1)
    dy_near, small = lax.optimization_barrier((dy_near, small))
    dy_far = pass_on(*dy_near)
    dh_near, grads_near, small = block(in_near, dy_near, mids_near, weights, small, 2)
    in_far, small = lax.optimization_barrier((in_far, small))
    (mids_far,) = hidden([in_far], w0, w1)
    (dh_far,), grads_far, small = block(in_far, dy_far, mids_far, weights, small, 1, TAIL)
    back_near = [shift(dh_near[0], "dp", -1), shift(dh_near[1], "dp", 1)]
    back_far = shift(dh_far, "dp", 2)
    smalls = [small, shift(small, "dp", 1), shift(small, "dp", -1)]

    grads = (*grads_own, *grads_near, *grads_far)
    rows, units = sum(part.shape[0] for part in grads[0::3]), w0.shape[1]
    grad_w0, grad_w1 = weight_grads(
        in_grads_kernel,
        [in_own] + in_near + in_far,
        [part for k, part in enumerate(grads) if k % 3],
        [w0.shape, w1.shape],
        (rows, 2 * units),
    )
    acts, back_near = lax.optimization_barrier((grads[0::3], back_near))
    (grad_wout,) = weight_grads(
        out_grad_kernel, [dy_own] + dy_near + dy_far, list(acts), [wo.shape], (units, rows)
    )
    back_far, grad_w0, grad_w1, grad_wout = lax.optimization_barrier(
        (back_far, grad_w0, grad_w1, grad_wout)
    )

    back = expand(dh_own, *back_near, back_far, home, slots, *smalls)
    back = exchange(back.reshape(experts, slots, -1)).reshape(total, -1)
    d_tokens, d_gain, d_router = finish(
        back, picker, tokens, grad_out, norm_gain.reshape(1, width), experts
    )
    return (
        d_tokens,
        d_gain.reshape(width),
        d_router.T,
        grad_w0[None],
        grad_w1[None],
        grad_wout[None],
    )


def solution(mesh):
    in_specs = (
        P(("dp", "expert"), None),
        P(("dp", "expert"), None),
        P(),
        P(),
        P("expert", None, "dp"),
        P("expert", None, "dp"),
        P("expert", "dp", None),
        P(("dp", "expert"), None, None),
        P(("dp", "expert"), None),
    )
    out_specs = (
        P(("dp", "expert"), None),
        P(),
        P(),
        P("expert", None, "dp"),
        P("expert", None, "dp"),
        P("expert", "dp", None),
    )
    return jax.shard_map(
        per_device, mesh=mesh, in_specs=in_specs, out_specs=out_specs, check_vma=False
    )
```

```python
import functools

import jax
import jax.numpy as jnp
from jax import lax
from jax.experimental import pallas as pl
from jax.experimental.pallas import tpu as pltpu
from jax.sharding import PartitionSpec as P

F32 = jnp.float32
BF16 = jnp.bfloat16
DEAD = 2.0**100
GELU_SCALE = 0.7978845608028654
GELU_CUBIC = 0.044715


def dot(a, b, dims=((1,), (0,))):
    return lax.dot_general(a, b, (dims, ((), ())), preferred_element_type=F32)


WHOLE = pl.BlockSpec(memory_space=pltpu.VMEM)
PARAMS = pltpu.CompilerParams(vmem_limit_bytes=24 * 1024 * 1024)
TAIL = 16
COST = pl.CostEstimate(flops=1, bytes_accessed=1, transcendentals=0)


def stack(values):
    return values[0] if len(values) == 1 else jnp.concatenate(values, axis=0)


def iota(shape, axis):
    return lax.broadcasted_iota(jnp.int32, shape, axis)


def one_hot_of_slots(slot_rows_ref, count_ref, tok_dev, copies):
    slots, experts = slot_rows_ref.shape
    total = copies * slots * experts
    line = iota((total, 1), 0)
    mine = iota((total, experts), 1) == line // (copies * slots)
    names = dot(
        mine.astype(BF16), slot_rows_ref[...].astype(F32).astype(BF16), ((1,), (1,))
    )
    place = line % slots
    name = jnp.where(place == iota((total, slots), 1), names, 0.0)
    name = jnp.sum(name, axis=1, keepdims=True)
    count = jnp.where(mine, count_ref[...].astype(F32), 0.0)
    live = place.astype(F32) < jnp.sum(count, axis=1, keepdims=True)
    name = jnp.where(live, name, -1.0)
    return iota((total, tok_dev), 1).astype(F32) == name, live


def pick_kernel(tokens_ref, grad_ref, gain_ref, slot_rows_ref, count_ref, slots_ref, picker_ref):
    tok_dev = picker_ref.shape[1]
    slots = slot_rows_ref.shape[0]
    tok = tokens_ref[...].astype(F32)
    inv_rms = lax.rsqrt(jnp.mean(tok * tok, axis=1, keepdims=True) + 1e-06)
    normed = (tok * inv_rms * gain_ref[...]).astype(BF16)
    hot, live = one_hot_of_slots(slot_rows_ref, count_ref, tok_dev, 2)
    second = iota((hot.shape[0], 1), 0) // slots % 2 == 1
    both = jnp.concatenate([hot & ~second, hot & second], axis=1).astype(BF16)
    rows = dot(both, jnp.concatenate([normed, grad_ref[...]], axis=0))
    slots_ref[...] = rows.astype(BF16)
    slots_ref[:, :128] = jnp.where(live, rows[:, :128], DEAD).astype(BF16)
    hot, _ = one_hot_of_slots(slot_rows_ref, count_ref, tok_dev, 1)
    picker_ref[...] = hot.astype(BF16)


def pick(tokens, grad_out, norm_gain, slot_rows, slot_count):
    total = slot_rows.shape[0] * slot_rows.shape[1]
    tok_dev, width = tokens.shape
    return pl.pallas_call(
        pick_kernel,
        out_shape=(
            jax.ShapeDtypeStruct((2 * total, width), BF16),
            jax.ShapeDtypeStruct((total, tok_dev), BF16),
        ),
        in_specs=[WHOLE] * 5,
        out_specs=[WHOLE] * 2,
        compiler_params=pltpu.CompilerParams(vmem_limit_bytes=56 * 1024 * 1024),
        cost_estimate=COST,
        name="pick",
    )(tokens, grad_out, norm_gain, slot_rows, slot_count)


def pack_kernel(slots, rows_ref, first_ref, second_ref, home_ref):
    both = rows_ref.shape[0]
    total, live_rows = home_ref.shape
    half = live_rows // 2
    line = iota((both, 1), 0)
    kind = line // slots % 2
    other = iota((1, both), 1)
    earlier = (other < line) & (other // slots % 2 == kind)
    alive = rows_ref[:, :1].astype(F32) < DEAD / 2
    flags = jnp.broadcast_to(alive.astype(F32), (both, live_rows)).astype(BF16)
    index = dot(earlier.astype(BF16), flags)
    hot = (index == iota((both, live_rows), 1).astype(F32)) & alive
    home = jnp.concatenate([hot & (kind == 0), hot & (kind == 1)], axis=1).astype(BF16)
    live = dot(home, rows_ref[...], ((0,), (0,))).astype(BF16)
    first_ref[:half, :] = live[:half]
    first_ref[half:, :] = live[live_rows : live_rows + half]
    second_ref[:half, :] = live[half:live_rows]
    second_ref[half:, :] = live[live_rows + half :]
    slot = iota((total, 1), 0)
    source = slot // slots * (2 * slots) + slot % slots
    mine = (iota((total, both), 1) == source).astype(BF16)
    home_ref[...] = dot(mine, home[:, :live_rows]).astype(BF16)


def pack(rows, slots):
    both, width = rows.shape
    total = both // 2
    return pl.pallas_call(
        functools.partial(pack_kernel, slots),
        out_shape=(
            jax.ShapeDtypeStruct((total // 2, width), BF16),
            jax.ShapeDtypeStruct((total // 2, width), BF16),
            jax.ShapeDtypeStruct((total, total // 2), BF16),
        ),
        in_specs=[WHOLE],
        out_specs=[WHOLE] * 3,
        compiler_params=PARAMS,
        cost_estimate=COST,
        name="pack",
    )(rows)


def hidden_kernel(n, *refs):
    w0_ref, w1_ref = refs[n : n + 2]
    outs = refs[n + 2 :]
    half = refs[0].shape[0] // 2
    rows = stack([ref[:half, :] for ref in refs[:n]])
    pre0 = dot(rows, w0_ref[...])
    pre1 = dot(rows, w1_ref[...])
    square = pre0 * pre0
    tanh = jnp.tanh(GELU_SCALE * pre0 * (1.0 + GELU_CUBIC * square))
    cdf = 0.5 + 0.5 * tanh
    slope = cdf + 0.5 * pre0 * (1.0 - tanh * tanh) * (
        GELU_SCALE * (1.0 + 3.0 * GELU_CUBIC * square)
    )
    gelu = pre0 * cdf
    mix = pre1 * slope
    act = gelu * pre1
    size = outs[0].shape[0]
    for k in range(len(outs) // 3):
        at = slice(k * size, (k + 1) * size)
        outs[3 * k][...] = gelu[at]
        outs[3 * k + 1][...] = mix[at]
        outs[3 * k + 2][...] = act[at]


def hidden(sets, w0, w1):
    width, units = w0.shape
    parts = [part for each in sets for part in each]
    m = len(sets[0]) * parts[0].shape[0] // 2
    flat = pl.pallas_call(
        functools.partial(hidden_kernel, len(parts)),
        out_shape=[jax.ShapeDtypeStruct((m, units), F32)] * (3 * len(sets)),
        in_specs=[WHOLE] * (len(parts) + 2),
        out_specs=[WHOLE] * (3 * len(sets)),
        compiler_params=PARAMS,
        cost_estimate=COST,
        name="hidden",
    )(*parts, w0, w1)
    return [flat[3 * k : 3 * k + 3] for k in range(len(sets))]


def block_kernel(n, sets, places, *refs):
    part_refs, mid_refs, refs = refs[:n], refs[n : n + 3 * sets], refs[n + 3 * sets :]
    w0_ref, w1_ref, wo_ref, rrow_ref, before_ref = refs[:5]
    *dh_refs, act_ref, d0_ref, d1_ref, small_ref = refs[5:]
    half = part_refs[0].shape[0] // 2
    gelu, mix, act = (stack([ref[...] for ref in mid_refs[k::3]]) for k in range(3))
    rrow = rrow_ref[...]
    up = dot(stack([ref[half:, :] for ref in part_refs]), wo_ref[...], ((1,), (1,)))
    rows32 = stack([ref[:half, :] for ref in part_refs]).astype(F32)
    logit = jnp.sum(rows32 * rrow, axis=1, keepdims=True)
    gate = 1.0 / (1.0 + jnp.exp(-logit))
    gate_row = gate.astype(BF16).astype(F32)
    dgate = jnp.sum(act * up, axis=1, keepdims=True)
    d_act = gate_row * up
    d0 = (d_act * mix).astype(BF16)
    d1 = (d_act * gelu).astype(BF16)
    act_ref[...] = (gate_row * act).astype(BF16)
    d0_ref[...] = d0
    d1_ref[...] = d1
    dlogit = dgate * gate * (1.0 - gate)
    dh = dot(d0, w0_ref[...], ((1,), (1,))) + dot(d1, w1_ref[...], ((1,), (1,)))
    dh = dh + dlogit * rrow
    col = jnp.sum(rows32 * dlogit, axis=0, keepdims=True)
    gain = jnp.sum(rows32 * dh, axis=0, keepdims=True)
    small = before_ref[...] + jnp.concatenate([col, gain], axis=0)
    small_ref[...] = small
    for k, (which, at) in enumerate(places):
        dh_refs[which][at * half : (at + 1) * half, :] = dh[k * half : (k + 1) * half].astype(BF16)
    for ref in dh_refs:
        if ref.shape[0] > 2 * half:
            high = small.astype(BF16)
            low = (small - high.astype(F32)).astype(BF16)
            rest = jnp.zeros((TAIL - 4, small.shape[1]), BF16)
            ref[2 * half :, :] = jnp.concatenate([high, low, rest], axis=0)


def block(parts, mids, weights, before, places, tail=0):
    width, units = weights[0].shape
    half = parts[0].shape[0] // 2
    m = half * len(parts)
    outs_n = len(parts) // 2
    flat = pl.pallas_call(
        functools.partial(block_kernel, len(parts), len(mids), places),
        out_shape=[jax.ShapeDtypeStruct((2 * half + tail, width), BF16)] * outs_n
        + [jax.ShapeDtypeStruct((m, units), BF16)] * 3
        + [jax.ShapeDtypeStruct((2, width), F32)],
        in_specs=[WHOLE] * (len(parts) + 3 * len(mids) + 5),
        out_specs=[WHOLE] * (outs_n + 4),
        compiler_params=PARAMS,
        cost_estimate=COST,
        name="block",
    )(*parts, *[value for mid in mids for value in mid], *weights, before)
    return flat[:outs_n], flat[outs_n : outs_n + 3], flat[-1]


def total_kernel(*refs):
    *part_refs, out_ref = refs
    out_ref[...] = sum(ref[...].astype(F32) for ref in part_refs)


def total_of(parts):
    return pl.pallas_call(
        total_kernel,
        out_shape=jax.ShapeDtypeStruct(parts[0].shape, F32),
        in_specs=[WHOLE] * len(parts),
        out_specs=WHOLE,
        compiler_params=PARAMS,
        cost_estimate=pl.CostEstimate(flops=1000000000, bytes_accessed=1, transcendentals=0),
        name="total_of",
    )(*parts)


def expand_kernel(dh_ref, far_ref, home_ref, small_ref, *refs):
    *others, out_ref = refs
    rows, width = dh_ref.shape
    dh = dh_ref[...] + far_ref[:rows, :].astype(F32)
    out_ref[:, :width] = dot(home_ref[...], dh.astype(BF16)).astype(BF16)
    carried = far_ref[rows:, :].astype(F32)
    small = small_ref[...] + carried[0:2] + carried[2:4]
    for ref in others:
        small = small + ref[...]
    part = out_ref.shape[1] - width
    lines = [small[k : k + 1, at : at + part] for k in range(2) for at in range(0, width, part)]
    lines = jnp.concatenate(lines, axis=0).astype(BF16)
    out_ref[:, width:] = jnp.concatenate([lines] * (out_ref.shape[0] // lines.shape[0]), axis=0)


def expand(dh, far, home, slots, *smalls):
    total = home.shape[0]
    width = dh.shape[1]
    return pl.pallas_call(
        expand_kernel,
        out_shape=jax.ShapeDtypeStruct((total, width + 2 * width // slots), BF16),
        in_specs=[WHOLE] * (3 + len(smalls)),
        out_specs=WHOLE,
        compiler_params=PARAMS,
        cost_estimate=COST,
        name="expand",
    )(dh, far, home, *smalls)


def finish_kernel(
    back_ref, picker_ref, tokens_ref, grad_ref, gain_ref, d_tokens_ref, d_gain_ref, d_router_ref
):
    total = back_ref.shape[0]
    width = tokens_ref.shape[1]
    experts = d_router_ref.shape[0]
    slots = total // experts
    half = slots // 2
    part = back_ref.shape[1] - width
    gain = gain_ref[...]
    tok = tokens_ref[...].astype(F32)
    inv_rms = lax.rsqrt(jnp.mean(tok * tok, axis=1, keepdims=True) + 1e-06)
    d_normed = dot(picker_ref[...], back_ref[:, :width], ((0,), (0,)))
    scaled = d_normed * gain
    inner = jnp.mean(scaled * tok, axis=1, keepdims=True)
    d_tokens_ref[...] = (
        grad_ref[...].astype(F32) + inv_rms * scaled - tok * (inv_rms * inv_rms * inv_rms * inner)
    ).astype(BF16)
    extra = back_ref[:, width:]
    slot = lax.broadcasted_iota(jnp.int32, (experts, total), 1)
    home = slots * lax.broadcasted_iota(jnp.int32, (experts, total), 0)
    place = lax.broadcasted_iota(jnp.int32, (slots, total), 1) % slots
    line = lax.broadcasted_iota(jnp.int32, (slots, total), 0)
    sums = dot((place == line).astype(BF16), extra)
    for q in range(half):
        at = slice(q * part, (q + 1) * part)
        d_router_ref[:, at] = dot((slot == home + q).astype(BF16), extra)
        d_gain_ref[:, at] = sums[half + q : half + q + 1, :] / gain[:, at]


def finish(back, picker, tokens, grad_out, norm_gain, experts):
    width = tokens.shape[1]
    return pl.pallas_call(
        finish_kernel,
        out_shape=(
            jax.ShapeDtypeStruct(tokens.shape, BF16),
            jax.ShapeDtypeStruct((1, width), F32),
            jax.ShapeDtypeStruct((experts, width), F32),
        ),
        in_specs=[WHOLE] * 5,
        out_specs=[WHOLE] * 3,
        compiler_params=PARAMS,
        cost_estimate=COST,
        name="finish",
    )(back, picker, tokens, grad_out, norm_gain)


def in_grads_kernel(n, *refs):
    w0_ref, w1_ref, pair_ref = refs[-3:]
    grads = refs[n:-3]
    units = w0_ref.shape[1]

    @pl.when(pl.program_id(0) == 0)
    def _():
        pair_ref[:, :units] = stack([ref[...] for ref in grads[0::2]])
        pair_ref[:, units:] = stack([ref[...] for ref in grads[1::2]])

    pair = dot(stack([ref[...] for ref in refs[:n]]), pair_ref[...], ((0,), (0,)))
    w0_ref[...] = pair[:, :units].astype(BF16)
    w1_ref[...] = pair[:, units:].astype(BF16)


def out_grad_kernel(n, *refs):
    wo_ref, act_ref = refs[-2:]

    @pl.when(pl.program_id(0) == 0)
    def _():
        act_ref[...] = stack([ref[...] for ref in refs[n:-2]]).T

    wo_ref[...] = dot(act_ref[...], stack([ref[...] for ref in refs[:n]])).astype(BF16)


def weight_grads(kernel, parts, which, factors, outs, scratch, tile=512):
    half, width = parts[0].shape[0] // 2, parts[0].shape[1]
    return pl.pallas_call(
        functools.partial(kernel, len(parts)),
        grid=(width // tile,),
        out_shape=[jax.ShapeDtypeStruct(shape, BF16) for shape in outs],
        in_specs=[pl.BlockSpec((half, tile), lambda i: (which, i))] * len(parts)
        + [pl.BlockSpec(value.shape, lambda i: (0, 0)) for value in factors],
        out_specs=[
            pl.BlockSpec((tile, shape[1]), lambda i: (i, 0))
            if shape[0] == width
            else pl.BlockSpec((shape[0], tile), lambda i: (0, i))
            for shape in outs
        ],
        scratch_shapes=[pltpu.VMEM(scratch, BF16)],
        compiler_params=PARAMS,
        cost_estimate=pl.CostEstimate(flops=2000000000, bytes_accessed=1, transcendentals=0),
        name="weight_grads",
    )(*parts, *factors)


def shift(value, axis, by):
    n = lax.axis_size(axis)
    return lax.ppermute(value, axis, [(i, (i + by) % n) for i in range(n)])


def exchange(value):
    return lax.all_to_all(value, "expert", split_axis=0, concat_axis=0, tiled=True)


def per_device(tokens, grad_out, norm_gain, router, w_in0, w_in1, w_out, slot_rows, slot_count):
    tok_dev, width = tokens.shape
    experts = router.shape[1]
    slots = slot_rows.shape[2]
    total = experts * slots
    w0, w1, wo = w_in0[0], w_in1[0], w_out[0]

    expert = lax.axis_index("expert")
    rrow = lax.dynamic_slice_in_dim(router.T, expert, 1, axis=0).astype(F32)
    both, picker = pick(
        tokens, grad_out, norm_gain.reshape(1, width), slot_rows[0].T, slot_count
    )
    both = exchange(both.reshape(experts, 2 * slots, width)).reshape(2 * total, width)
    both, rrow = lax.optimization_barrier((both, rrow))
    first, second, home = pack(both, slots)
    weights = (w0, w1, wo, rrow)
    early = [shift(first, "dp", 1), shift(second, "dp", -1)]
    late = [shift(second, "dp", 1), shift(first, "dp", -1)]
    far = [shift(early[0], "dp", 1), shift(early[1], "dp", -1)]
    one = ((0, 0), (0, 1))
    mid_own, mid_early = hidden([[first, second], early], w0, w1)
    small = jnp.zeros((2, width), F32)
    (dh_own,), grads_own, small = block([first, second], [mid_own], weights, small, one)
    late, small = lax.optimization_barrier((late, small))
    (mid_late,) = hidden([late], w0, w1)
    dh_near, grads_near, small = block(
        early + late, [mid_early, mid_late], weights, small, ((0, 0), (1, 1), (0, 1), (1, 0))
    )
    far, small = lax.optimization_barrier((far, small))
    (mid_far,) = hidden([far], w0, w1)
    (dh_far,), grads_far, small = block(far, [mid_far], weights, small, one, TAIL)
    back_near = [shift(dh_near[0], "dp", -1), shift(dh_near[1], "dp", 1)]
    back_far = shift(dh_far, "dp", 2)
    smalls = [small, shift(small, "dp", 1), shift(small, "dp", -1)]

    parts = [first, second] + early + late + far
    grads = (*grads_own, *grads_near, *grads_far)
    rows, units = 4 * first.shape[0], w0.shape[1]
    grad_w0, grad_w1 = weight_grads(
        in_grads_kernel,
        parts,
        0,
        [part for k, part in enumerate(grads) if k % 3],
        [w0.shape, w1.shape],
        (rows, 2 * units),
    )
    (grad_wout,) = weight_grads(
        out_grad_kernel, parts, 1, list(grads[0::3]), [wo.shape], (units, rows)
    )
    back_far, grad_w0, grad_w1, grad_wout = lax.optimization_barrier(
        (back_far, grad_w0, grad_w1, grad_wout)
    )

    back = expand(total_of([dh_own, *back_near]), back_far, home, slots, *smalls)
    back = exchange(back.reshape(experts, slots, -1)).reshape(total, -1)
    d_tokens, d_gain, d_router = finish(
        back, picker, tokens, grad_out, norm_gain.reshape(1, width), experts
    )
    return (
        d_tokens,
        d_gain.reshape(width),
        d_router.T,
        grad_w0[None],
        grad_w1[None],
        grad_wout[None],
    )


def solution(mesh):
    in_specs = (
        P(("dp", "expert"), None),
        P(("dp", "expert"), None),
        P(),
        P(),
        P("expert", None, "dp"),
        P("expert", None, "dp"),
        P("expert", "dp", None),
        P(("dp", "expert"), None, None),
        P(("dp", "expert"), None),
    )
    out_specs = (
        P(("dp", "expert"), None),
        P(),
        P(),
        P("expert", None, "dp"),
        P("expert", None, "dp"),
        P("expert", "dp", None),
    )
    return jax.shard_map(
        per_device, mesh=mesh, in_specs=in_specs, out_specs=out_specs, check_vma=False
    )
```

```python
import functools

import jax
import jax.numpy as jnp
from jax import lax
from jax.experimental import pallas as pl
from jax.experimental.pallas import tpu as pltpu
from jax.sharding import PartitionSpec as P

F32 = jnp.float32
BF16 = jnp.bfloat16
DEAD = 2.0**100
GELU_SCALE = 0.7978845608028654
GELU_CUBIC = 0.044715


def dot(a, b, dims=((1,), (0,))):
    return lax.dot_general(a, b, (dims, ((), ())), preferred_element_type=F32)


WHOLE = pl.BlockSpec(memory_space=pltpu.VMEM)
PARAMS = pltpu.CompilerParams(vmem_limit_bytes=24 * 1024 * 1024)
TAIL = 128
COST = pl.CostEstimate(flops=1, bytes_accessed=1, transcendentals=0)


def stack(values):
    return values[0] if len(values) == 1 else jnp.concatenate(values, axis=0)


def iota(shape, axis):
    return lax.broadcasted_iota(jnp.int32, shape, axis)


def one_hot_of_slots(slot_rows_ref, count_ref, tok_dev, copies):
    slots, experts = slot_rows_ref.shape
    total = copies * slots * experts
    line = iota((total, 1), 0)
    mine = iota((total, experts), 1) == line // (copies * slots)
    names = dot(
        mine.astype(BF16), slot_rows_ref[...].astype(F32).astype(BF16), ((1,), (1,))
    )
    place = line % slots
    name = jnp.where(place == iota((total, slots), 1), names, 0.0)
    name = jnp.sum(name, axis=1, keepdims=True)
    count = jnp.where(mine, count_ref[...].astype(F32), 0.0)
    live = place.astype(F32) < jnp.sum(count, axis=1, keepdims=True)
    name = jnp.where(live, name, -1.0)
    return iota((total, tok_dev), 1).astype(F32) == name, live


def pick_kernel(tokens_ref, grad_ref, gain_ref, slot_rows_ref, count_ref, slots_ref, picker_ref):
    tok_dev = picker_ref.shape[1]
    slots = slot_rows_ref.shape[0]
    tok = tokens_ref[...].astype(F32)
    inv_rms = lax.rsqrt(jnp.mean(tok * tok, axis=1, keepdims=True) + 1e-06)
    normed = (tok * inv_rms * gain_ref[...]).astype(BF16)
    hot, live = one_hot_of_slots(slot_rows_ref, count_ref, tok_dev, 2)
    second = iota((hot.shape[0], 1), 0) // slots % 2 == 1
    both = jnp.concatenate([hot & ~second, hot & second], axis=1).astype(BF16)
    rows = dot(both, jnp.concatenate([normed, grad_ref[...]], axis=0))
    slots_ref[...] = rows.astype(BF16)
    slots_ref[:, :128] = jnp.where(live, rows[:, :128], DEAD).astype(BF16)
    hot, _ = one_hot_of_slots(slot_rows_ref, count_ref, tok_dev, 1)
    picker_ref[...] = hot.astype(BF16)


def pick(tokens, grad_out, norm_gain, slot_rows, slot_count):
    total = slot_rows.shape[0] * slot_rows.shape[1]
    tok_dev, width = tokens.shape
    return pl.pallas_call(
        pick_kernel,
        out_shape=(
            jax.ShapeDtypeStruct((2 * total, width), BF16),
            jax.ShapeDtypeStruct((total, tok_dev), BF16),
        ),
        in_specs=[WHOLE] * 5,
        out_specs=[WHOLE] * 2,
        compiler_params=pltpu.CompilerParams(vmem_limit_bytes=56 * 1024 * 1024),
        cost_estimate=COST,
        name="pick",
    )(tokens, grad_out, norm_gain, slot_rows, slot_count)


def pack_kernel(slots, rows_ref, first_ref, second_ref, home_ref):
    both = rows_ref.shape[0]
    total, live_rows = home_ref.shape
    half = live_rows // 2
    line = iota((both, 1), 0)
    kind = line // slots % 2
    other = iota((1, both), 1)
    earlier = (other < line) & (other // slots % 2 == kind)
    alive = rows_ref[:, :1].astype(F32) < DEAD / 2
    flags = jnp.broadcast_to(alive.astype(F32), (both, live_rows)).astype(BF16)
    index = dot(earlier.astype(BF16), flags)
    hot = (index == iota((both, live_rows), 1).astype(F32)) & alive
    home = jnp.concatenate([hot & (kind == 0), hot & (kind == 1)], axis=1).astype(BF16)
    live = dot(home, rows_ref[...], ((0,), (0,))).astype(BF16)
    first_ref[:half, :] = live[:half]
    first_ref[half:, :] = live[live_rows : live_rows + half]
    second_ref[:half, :] = live[half:live_rows]
    second_ref[half:, :] = live[live_rows + half :]
    slot = iota((total, 1), 0)
    source = slot // slots * (2 * slots) + slot % slots
    mine = (iota((total, both), 1) == source).astype(BF16)
    home_ref[...] = dot(mine, home[:, :live_rows]).astype(BF16)


def pack(rows, slots):
    both, width = rows.shape
    total = both // 2
    return pl.pallas_call(
        functools.partial(pack_kernel, slots),
        out_shape=(
            jax.ShapeDtypeStruct((total // 2, width), BF16),
            jax.ShapeDtypeStruct((total // 2, width), BF16),
            jax.ShapeDtypeStruct((total, total // 2), BF16),
        ),
        in_specs=[WHOLE],
        out_specs=[WHOLE] * 3,
        compiler_params=PARAMS,
        cost_estimate=COST,
        name="pack",
    )(rows)


def hidden_kernel(n, *refs):
    w0_ref, w1_ref = refs[n : n + 2]
    outs = refs[n + 2 :]
    half = refs[0].shape[0] // 2
    rows = stack([ref[:half, :] for ref in refs[:n]])
    pre0 = dot(rows, w0_ref[...])
    pre1 = dot(rows, w1_ref[...])
    square = pre0 * pre0
    tanh = jnp.tanh(GELU_SCALE * pre0 * (1.0 + GELU_CUBIC * square))
    cdf = 0.5 + 0.5 * tanh
    slope = cdf + 0.5 * pre0 * (1.0 - tanh * tanh) * (
        GELU_SCALE * (1.0 + 3.0 * GELU_CUBIC * square)
    )
    gelu = pre0 * cdf
    mix = pre1 * slope
    act = gelu * pre1
    size = outs[0].shape[0]
    for k in range(len(outs) // 3):
        at = slice(k * size, (k + 1) * size)
        outs[3 * k][...] = gelu[at]
        outs[3 * k + 1][...] = mix[at]
        outs[3 * k + 2][...] = act[at]


def hidden(sets, w0, w1):
    width, units = w0.shape
    parts = [part for each in sets for part in each]
    m = len(sets[0]) * parts[0].shape[0] // 2
    flat = pl.pallas_call(
        functools.partial(hidden_kernel, len(parts)),
        out_shape=[jax.ShapeDtypeStruct((m, units), F32)] * (3 * len(sets)),
        in_specs=[WHOLE] * (len(parts) + 2),
        out_specs=[WHOLE] * (3 * len(sets)),
        compiler_params=PARAMS,
        cost_estimate=COST,
        name="hidden",
    )(*parts, w0, w1)
    return [flat[3 * k : 3 * k + 3] for k in range(len(sets))]


def lined(sums, part):
    width = sums.shape[1]
    return stack([sums[k : k + 1, at : at + part] for k in range(2) for at in range(0, width, part)])


def block_kernel(n, sets, places, *refs):
    part_refs, mid_refs, refs = refs[:n], refs[n : n + 3 * sets], refs[n + 3 * sets :]
    w0_ref, w1_ref, wo_ref, rrow_ref, before_ref = refs[:5]
    *dh_refs, act_ref, d0_ref, d1_ref, small_ref = refs[5:]
    half = part_refs[0].shape[0] // 2
    gelu, mix, act = (stack([ref[...] for ref in mid_refs[k::3]]) for k in range(3))
    rrow = rrow_ref[...]
    up = dot(stack([ref[half:, :] for ref in part_refs]), wo_ref[...], ((1,), (1,)))
    rows32 = stack([ref[:half, :] for ref in part_refs]).astype(F32)
    logit = jnp.sum(rows32 * rrow, axis=1, keepdims=True)
    gate = 1.0 / (1.0 + jnp.exp(-logit))
    gate_row = gate.astype(BF16).astype(F32)
    dgate = jnp.sum(act * up, axis=1, keepdims=True)
    d_act = gate_row * up
    d0 = (d_act * mix).astype(BF16)
    d1 = (d_act * gelu).astype(BF16)
    act_ref[...] = (gate_row * act).astype(BF16)
    d0_ref[...] = d0
    d1_ref[...] = d1
    dlogit = dgate * gate * (1.0 - gate)
    dh = dot(d0, w0_ref[...], ((1,), (1,))) + dot(d1, w1_ref[...], ((1,), (1,)))
    dh = dh + dlogit * rrow
    col = jnp.sum(rows32 * dlogit, axis=0, keepdims=True)
    gain = jnp.sum(rows32 * dh, axis=0, keepdims=True)
    small = before_ref[...] + jnp.concatenate([col, gain], axis=0)
    small_ref[...] = small
    for k, (which, at) in enumerate(places):
        lines = dh[k * half : (k + 1) * half].astype(BF16)
        dh_refs[which][at * half : (at + 1) * half, : dh.shape[1]] = lines
    for ref in dh_refs:
        if ref.shape[1] > dh.shape[1]:
            high = small.astype(BF16).astype(F32)
            lines = [lined(value, TAIL) for value in (high, small - high)]
            rest = ref.shape[0] - 2 * lines[0].shape[0]
            lines.append(jnp.zeros((rest, TAIL), F32))
            ref[:, dh.shape[1] :] = stack(lines).astype(BF16)


def block(parts, mids, weights, before, places, tail=0):
    width, units = weights[0].shape
    half = parts[0].shape[0] // 2
    m = half * len(parts)
    outs_n = len(parts) // 2
    flat = pl.pallas_call(
        functools.partial(block_kernel, len(parts), len(mids), places),
        out_shape=[jax.ShapeDtypeStruct((2 * half, width + tail), BF16)] * outs_n
        + [jax.ShapeDtypeStruct((m, units), BF16)] * 3
        + [jax.ShapeDtypeStruct((2, width), F32)],
        in_specs=[WHOLE] * (len(parts) + 3 * len(mids) + 5),
        out_specs=[WHOLE] * (outs_n + 4),
        compiler_params=PARAMS,
        cost_estimate=COST,
        name="block",
    )(*parts, *[value for mid in mids for value in mid], *weights, before)
    return flat[:outs_n], flat[outs_n : outs_n + 3], flat[-1]


def total_kernel(*refs):
    *part_refs, out_ref = refs
    out_ref[...] = sum(ref[...].astype(F32) for ref in part_refs)


def total_of(parts):
    return pl.pallas_call(
        total_kernel,
        out_shape=jax.ShapeDtypeStruct(parts[0].shape, F32),
        in_specs=[WHOLE] * len(parts),
        out_specs=WHOLE,
        compiler_params=PARAMS,
        cost_estimate=pl.CostEstimate(flops=1000000000, bytes_accessed=1, transcendentals=0),
        name="total_of",
    )(*parts)


def expand_kernel(dh_ref, far_ref, home_ref, small_ref, *refs):
    *others, out_ref = refs
    rows, width = dh_ref.shape
    dh = dh_ref[...] + far_ref[:, :width].astype(F32)
    out_ref[:, :width] = dot(home_ref[...], dh.astype(BF16)).astype(BF16)
    small = small_ref[...]
    for ref in others:
        small = small + ref[...]
    part = out_ref.shape[1] - width
    lines = lined(small, part)
    count = 2 * width // TAIL
    carried = far_ref[:, width:].astype(F32)
    carried = carried[:count] + carried[count : 2 * count]
    each = part // TAIL
    pieces = [
        jnp.concatenate([carried[q * each + k : q * each + k + 1] for k in range(each)], axis=1)
        for q in range(lines.shape[0])
    ]
    lines = (lines + stack(pieces)).astype(BF16)
    out_ref[:, width:] = jnp.concatenate([lines] * (out_ref.shape[0] // lines.shape[0]), axis=0)


def expand(dh, far, home, slots, *smalls):
    total = home.shape[0]
    width = dh.shape[1]
    return pl.pallas_call(
        expand_kernel,
        out_shape=jax.ShapeDtypeStruct((total, width + 2 * width // slots), BF16),
        in_specs=[WHOLE] * (3 + len(smalls)),
        out_specs=WHOLE,
        compiler_params=PARAMS,
        cost_estimate=COST,
        name="expand",
    )(dh, far, home, *smalls)


def finish_kernel(
    back_ref, picker_ref, tokens_ref, grad_ref, gain_ref, d_tokens_ref, d_gain_ref, d_router_ref
):
    total = back_ref.shape[0]
    width = tokens_ref.shape[1]
    experts = d_router_ref.shape[0]
    slots = total // experts
    half = slots // 2
    part = back_ref.shape[1] - width
    gain = gain_ref[...]
    tok = tokens_ref[...].astype(F32)
    inv_rms = lax.rsqrt(jnp.mean(tok * tok, axis=1, keepdims=True) + 1e-06)
    d_normed = dot(picker_ref[...], back_ref[:, :width], ((0,), (0,)))
    scaled = d_normed * gain
    inner = jnp.mean(scaled * tok, axis=1, keepdims=True)
    d_tokens_ref[...] = (
        grad_ref[...].astype(F32) + inv_rms * scaled - tok * (inv_rms * inv_rms * inv_rms * inner)
    ).astype(BF16)
    extra = back_ref[:, width:]
    slot = lax.broadcasted_iota(jnp.int32, (experts, total), 1)
    home = slots * lax.broadcasted_iota(jnp.int32, (experts, total), 0)
    place = lax.broadcasted_iota(jnp.int32, (slots, total), 1) % slots
    line = lax.broadcasted_iota(jnp.int32, (slots, total), 0)
    sums = dot((place == line).astype(BF16), extra)
    for q in range(half):
        at = slice(q * part, (q + 1) * part)
        d_router_ref[:, at] = dot((slot == home + q).astype(BF16), extra)
        d_gain_ref[:, at] = sums[half + q : half + q + 1, :] / gain[:, at]


def finish(back, picker, tokens, grad_out, norm_gain, experts):
    width = tokens.shape[1]
    return pl.pallas_call(
        finish_kernel,
        out_shape=(
            jax.ShapeDtypeStruct(tokens.shape, BF16),
            jax.ShapeDtypeStruct((1, width), F32),
            jax.ShapeDtypeStruct((experts, width), F32),
        ),
        in_specs=[WHOLE] * 5,
        out_specs=[WHOLE] * 3,
        compiler_params=PARAMS,
        cost_estimate=COST,
        name="finish",
    )(back, picker, tokens, grad_out, norm_gain)


def in_grads_kernel(n, *refs):
    w0_ref, w1_ref, pair_ref = refs[-3:]
    grads = refs[n:-3]
    units = w0_ref.shape[1]

    @pl.when(pl.program_id(0) == 0)
    def _():
        pair_ref[:, :units] = stack([ref[...] for ref in grads[0::2]])
        pair_ref[:, units:] = stack([ref[...] for ref in grads[1::2]])

    pair = dot(stack([ref[...] for ref in refs[:n]]), pair_ref[...], ((0,), (0,)))
    w0_ref[...] = pair[:, :units].astype(BF16)
    w1_ref[...] = pair[:, units:].astype(BF16)


def out_grad_kernel(n, *refs):
    wo_ref, act_ref = refs[-2:]

    @pl.when(pl.program_id(0) == 0)
    def _():
        act_ref[...] = stack([ref[...] for ref in refs[n:-2]]).T

    wo_ref[...] = dot(act_ref[...], stack([ref[...] for ref in refs[:n]])).astype(BF16)


def weight_grads(kernel, parts, which, factors, outs, scratch, tile=512):
    half, width = parts[0].shape[0] // 2, parts[0].shape[1]
    return pl.pallas_call(
        functools.partial(kernel, len(parts)),
        grid=(width // tile,),
        out_shape=[jax.ShapeDtypeStruct(shape, BF16) for shape in outs],
        in_specs=[pl.BlockSpec((half, tile), lambda i: (which, i))] * len(parts)
        + [pl.BlockSpec(value.shape, lambda i: (0, 0)) for value in factors],
        out_specs=[
            pl.BlockSpec((tile, shape[1]), lambda i: (i, 0))
            if shape[0] == width
            else pl.BlockSpec((shape[0], tile), lambda i: (0, i))
            for shape in outs
        ],
        scratch_shapes=[pltpu.VMEM(scratch, BF16)],
        compiler_params=PARAMS,
        cost_estimate=pl.CostEstimate(flops=2000000000, bytes_accessed=1, transcendentals=0),
        name="weight_grads",
    )(*parts, *factors)


def shift(value, axis, by):
    n = lax.axis_size(axis)
    return lax.ppermute(value, axis, [(i, (i + by) % n) for i in range(n)])


def exchange(value):
    return lax.all_to_all(value, "expert", split_axis=0, concat_axis=0, tiled=True)


def per_device(tokens, grad_out, norm_gain, router, w_in0, w_in1, w_out, slot_rows, slot_count):
    tok_dev, width = tokens.shape
    experts = router.shape[1]
    slots = slot_rows.shape[2]
    total = experts * slots
    w0, w1, wo = w_in0[0], w_in1[0], w_out[0]

    expert = lax.axis_index("expert")
    rrow = lax.dynamic_slice_in_dim(router.T, expert, 1, axis=0).astype(F32)
    both, picker = pick(
        tokens, grad_out, norm_gain.reshape(1, width), slot_rows[0].T, slot_count
    )
    both = exchange(both.reshape(experts, 2 * slots, width)).reshape(2 * total, width)
    both, rrow = lax.optimization_barrier((both, rrow))
    first, second, home = pack(both, slots)
    weights = (w0, w1, wo, rrow)
    early = [shift(first, "dp", 1), shift(second, "dp", -1)]
    late = [shift(second, "dp", 1), shift(first, "dp", -1)]
    far = [shift(early[0], "dp", 1), shift(early[1], "dp", -1)]
    one = ((0, 0), (0, 1))
    mid_own, mid_early = hidden([[first, second], early], w0, w1)
    small = jnp.zeros((2, width), F32)
    (dh_own,), grads_own, small = block([first, second], [mid_own], weights, small, one)
    late, small = lax.optimization_barrier((late, small))
    (mid_late,) = hidden([late], w0, w1)
    dh_near, grads_near, small = block(
        early + late, [mid_early, mid_late], weights, small, ((0, 0), (1, 1), (0, 1), (1, 0))
    )
    far, small = lax.optimization_barrier((far, small))
    (mid_far,) = hidden([far], w0, w1)
    (dh_far,), grads_far, small = block(far, [mid_far], weights, small, one, TAIL)
    back_near = [shift(dh_near[0], "dp", -1), shift(dh_near[1], "dp", 1)]
    back_far = shift(dh_far, "dp", 2)
    smalls = [small, shift(small, "dp", 1), shift(small, "dp", -1)]

    parts = [first, second] + early + late + far
    grads = (*grads_own, *grads_near, *grads_far)
    rows, units = 4 * first.shape[0], w0.shape[1]
    grad_w0, grad_w1 = weight_grads(
        in_grads_kernel,
        parts,
        0,
        [part for k, part in enumerate(grads) if k % 3],
        [w0.shape, w1.shape],
        (rows, 2 * units),
    )
    (grad_wout,) = weight_grads(
        out_grad_kernel, parts, 1, list(grads[0::3]), [wo.shape], (units, rows)
    )
    back_far, grad_w0, grad_w1, grad_wout = lax.optimization_barrier(
        (back_far, grad_w0, grad_w1, grad_wout)
    )

    back = expand(total_of([dh_own, *back_near]), back_far, home, slots, *smalls)
    back = exchange(back.reshape(experts, slots, -1)).reshape(total, -1)
    d_tokens, d_gain, d_router = finish(
        back, picker, tokens, grad_out, norm_gain.reshape(1, width), experts
    )
    return (
        d_tokens,
        d_gain.reshape(width),
        d_router.T,
        grad_w0[None],
        grad_w1[None],
        grad_wout[None],
    )


def solution(mesh):
    in_specs = (
        P(("dp", "expert"), None),
        P(("dp", "expert"), None),
        P(),
        P(),
        P("expert", None, "dp"),
        P("expert", None, "dp"),
        P("expert", "dp", None),
        P(("dp", "expert"), None, None),
        P(("dp", "expert"), None),
    )
    out_specs = (
        P(("dp", "expert"), None),
        P(),
        P(),
        P("expert", None, "dp"),
        P("expert", None, "dp"),
        P("expert", "dp", None),
    )
    return jax.shard_map(
        per_device, mesh=mesh, in_specs=in_specs, out_specs=out_specs, check_vma=False
    )
```

```python
import functools

import jax
import jax.numpy as jnp
from jax import lax
from jax.experimental import pallas as pl
from jax.experimental.pallas import tpu as pltpu
from jax.sharding import PartitionSpec as P

F32 = jnp.float32
BF16 = jnp.bfloat16
DEAD = 2.0**100
GELU_SCALE = 0.7978845608028654
GELU_CUBIC = 0.044715


def dot(a, b, dims=((1,), (0,))):
    return lax.dot_general(a, b, (dims, ((), ())), preferred_element_type=F32)


WHOLE = pl.BlockSpec(memory_space=pltpu.VMEM)
PARAMS = pltpu.CompilerParams(vmem_limit_bytes=24 * 1024 * 1024)
TAIL = 128
COST = pl.CostEstimate(flops=1, bytes_accessed=1, transcendentals=0)


def stack(values):
    return values[0] if len(values) == 1 else jnp.concatenate(values, axis=0)


def iota(shape, axis):
    return lax.broadcasted_iota(jnp.int32, shape, axis)


def one_hot_of_slots(slot_rows_ref, count_ref, tok_dev, copies):
    slots, experts = slot_rows_ref.shape
    total = copies * slots * experts
    line = iota((total, 1), 0)
    mine = iota((total, experts), 1) == line // (copies * slots)
    names = dot(
        mine.astype(BF16), slot_rows_ref[...].astype(F32).astype(BF16), ((1,), (1,))
    )
    place = line % slots
    name = jnp.where(place == iota((total, slots), 1), names, 0.0)
    name = jnp.sum(name, axis=1, keepdims=True)
    count = jnp.where(mine, count_ref[...].astype(F32), 0.0)
    live = place.astype(F32) < jnp.sum(count, axis=1, keepdims=True)
    name = jnp.where(live, name, -1.0)
    return iota((total, tok_dev), 1).astype(F32) == name, live


def pick_kernel(tokens_ref, grad_ref, gain_ref, slot_rows_ref, count_ref, slots_ref):
    tok_dev = tokens_ref.shape[0]
    slots = slot_rows_ref.shape[0]
    tok = tokens_ref[...].astype(F32)
    inv_rms = lax.rsqrt(jnp.mean(tok * tok, axis=1, keepdims=True) + 1e-06)
    normed = (tok * inv_rms * gain_ref[...]).astype(BF16)
    hot, live = one_hot_of_slots(slot_rows_ref, count_ref, tok_dev, 2)
    second = iota((hot.shape[0], 1), 0) // slots % 2 == 1
    both = jnp.concatenate([hot & ~second, hot & second], axis=1).astype(BF16)
    rows = dot(both, jnp.concatenate([normed, grad_ref[...]], axis=0))
    slots_ref[...] = rows.astype(BF16)
    slots_ref[:, :128] = jnp.where(live, rows[:, :128], DEAD).astype(BF16)


def pick(tokens, grad_out, norm_gain, slot_rows, slot_count):
    total = slot_rows.shape[0] * slot_rows.shape[1]
    tok_dev, width = tokens.shape
    return pl.pallas_call(
        pick_kernel,
        out_shape=jax.ShapeDtypeStruct((2 * total, width), BF16),
        in_specs=[WHOLE] * 5,
        out_specs=WHOLE,
        compiler_params=pltpu.CompilerParams(vmem_limit_bytes=56 * 1024 * 1024),
        cost_estimate=COST,
        name="pick",
    )(tokens, grad_out, norm_gain, slot_rows, slot_count)


def picker_kernel(slot_rows_ref, count_ref, picker_ref):
    hot, _ = one_hot_of_slots(slot_rows_ref, count_ref, picker_ref.shape[1], 1)
    picker_ref[...] = hot.astype(BF16)


def picker_of(slot_rows, slot_count, tok_dev):
    total = slot_rows.shape[0] * slot_rows.shape[1]
    return pl.pallas_call(
        picker_kernel,
        out_shape=jax.ShapeDtypeStruct((total, tok_dev), BF16),
        in_specs=[WHOLE] * 2,
        out_specs=WHOLE,
        compiler_params=PARAMS,
        cost_estimate=COST,
        name="picker_of",
    )(slot_rows, slot_count)


def home_kernel(slots, place_ref, home_ref):
    total, live_rows = home_ref.shape
    slot = iota((total, 1), 0)
    source = slot // slots * (2 * slots) + slot % slots
    mine = (iota((total, 2 * total), 1) == source).astype(BF16)
    home_ref[...] = dot(mine, place_ref[:, :live_rows]).astype(BF16)


def home_of(place, slots):
    both, total = place.shape
    return pl.pallas_call(
        functools.partial(home_kernel, slots),
        out_shape=jax.ShapeDtypeStruct((total, total // 2), BF16),
        in_specs=[WHOLE],
        out_specs=WHOLE,
        compiler_params=PARAMS,
        cost_estimate=COST,
        name="home_of",
    )(place)


def pack_kernel(slots, rows_ref, first_ref, second_ref, place_ref):
    both, total = place_ref.shape
    live_rows = total // 2
    half = live_rows // 2
    line = iota((both, 1), 0)
    kind = line // slots % 2
    other = iota((1, both), 1)
    earlier = (other < line) & (other // slots % 2 == kind)
    alive = rows_ref[:, :1].astype(F32) < DEAD / 2
    flags = jnp.broadcast_to(alive.astype(F32), (both, live_rows)).astype(BF16)
    index = dot(earlier.astype(BF16), flags)
    hot = (index == iota((both, live_rows), 1).astype(F32)) & alive
    home = jnp.concatenate([hot & (kind == 0), hot & (kind == 1)], axis=1).astype(BF16)
    live = dot(home, rows_ref[...], ((0,), (0,))).astype(BF16)
    first_ref[:half, :] = live[:half]
    first_ref[half:, :] = live[live_rows : live_rows + half]
    second_ref[:half, :] = live[half:live_rows]
    second_ref[half:, :] = live[live_rows + half :]
    place_ref[...] = home


def pack(rows, slots):
    both, width = rows.shape
    total = both // 2
    return pl.pallas_call(
        functools.partial(pack_kernel, slots),
        out_shape=(
            jax.ShapeDtypeStruct((total // 2, width), BF16),
            jax.ShapeDtypeStruct((total // 2, width), BF16),
            jax.ShapeDtypeStruct((both, total), BF16),
        ),
        in_specs=[WHOLE],
        out_specs=[WHOLE] * 3,
        compiler_params=PARAMS,
        cost_estimate=COST,
        name="pack",
    )(rows)


def hidden_kernel(n, *refs):
    w0_ref, w1_ref = refs[n : n + 2]
    outs = refs[n + 2 :]
    half = refs[0].shape[0] // 2
    rows = stack([ref[:half, :] for ref in refs[:n]])
    pre0 = dot(rows, w0_ref[...])
    pre1 = dot(rows, w1_ref[...])
    square = pre0 * pre0
    tanh = jnp.tanh(GELU_SCALE * pre0 * (1.0 + GELU_CUBIC * square))
    cdf = 0.5 + 0.5 * tanh
    slope = cdf + 0.5 * pre0 * (1.0 - tanh * tanh) * (
        GELU_SCALE * (1.0 + 3.0 * GELU_CUBIC * square)
    )
    gelu = pre0 * cdf
    mix = pre1 * slope
    act = gelu * pre1
    size = outs[0].shape[0]
    for k in range(len(outs) // 3):
        at = slice(k * size, (k + 1) * size)
        outs[3 * k][...] = gelu[at]
        outs[3 * k + 1][...] = mix[at]
        outs[3 * k + 2][...] = act[at]


def hidden(sets, w0, w1):
    width, units = w0.shape
    parts = [part for each in sets for part in each]
    m = len(sets[0]) * parts[0].shape[0] // 2
    flat = pl.pallas_call(
        functools.partial(hidden_kernel, len(parts)),
        out_shape=[jax.ShapeDtypeStruct((m, units), F32)] * (3 * len(sets)),
        in_specs=[WHOLE] * (len(parts) + 2),
        out_specs=[WHOLE] * (3 * len(sets)),
        compiler_params=PARAMS,
        cost_estimate=COST,
        name="hidden",
    )(*parts, w0, w1)
    return [flat[3 * k : 3 * k + 3] for k in range(len(sets))]


def lined(sums, part):
    width = sums.shape[1]
    return stack([sums[k : k + 1, at : at + part] for k in range(2) for at in range(0, width, part)])


def block_kernel(n, sets, places, *refs):
    part_refs, mid_refs, refs = refs[:n], refs[n : n + 3 * sets], refs[n + 3 * sets :]
    w0_ref, w1_ref, wo_ref, rrow_ref, before_ref = refs[:5]
    *dh_refs, act_ref, d0_ref, d1_ref, small_ref = refs[5:]
    half = part_refs[0].shape[0] // 2
    gelu, mix, act = (stack([ref[...] for ref in mid_refs[k::3]]) for k in range(3))
    rrow = rrow_ref[...]
    up = dot(stack([ref[half:, :] for ref in part_refs]), wo_ref[...], ((1,), (1,)))
    rows32 = stack([ref[:half, :] for ref in part_refs]).astype(F32)
    logit = jnp.sum(rows32 * rrow, axis=1, keepdims=True)
    gate = 1.0 / (1.0 + jnp.exp(-logit))
    gate_row = gate.astype(BF16).astype(F32)
    dgate = jnp.sum(act * up, axis=1, keepdims=True)
    d_act = gate_row * up
    d0 = (d_act * mix).astype(BF16)
    d1 = (d_act * gelu).astype(BF16)
    act_ref[...] = (gate_row * act).astype(BF16)
    d0_ref[...] = d0
    d1_ref[...] = d1
    dlogit = dgate * gate * (1.0 - gate)
    dh = dot(d0, w0_ref[...], ((1,), (1,))) + dot(d1, w1_ref[...], ((1,), (1,)))
    dh = dh + dlogit * rrow
    col = jnp.sum(rows32 * dlogit, axis=0, keepdims=True)
    gain = jnp.sum(rows32 * dh, axis=0, keepdims=True)
    small = before_ref[...] + jnp.concatenate([col, gain], axis=0)
    small_ref[...] = small
    for k, (which, at) in enumerate(places):
        lines = dh[k * half : (k + 1) * half].astype(BF16)
        dh_refs[which][at * half : (at + 1) * half, : dh.shape[1]] = lines
    for ref in dh_refs:
        if ref.shape[1] > dh.shape[1]:
            high = small.astype(BF16).astype(F32)
            lines = [lined(value, TAIL) for value in (high, small - high)]
            rest = ref.shape[0] - 2 * lines[0].shape[0]
            lines.append(jnp.zeros((rest, TAIL), F32))
            ref[:, dh.shape[1] :] = stack(lines).astype(BF16)


def block(parts, mids, weights, before, places, tail=0):
    width, units = weights[0].shape
    half = parts[0].shape[0] // 2
    m = half * len(parts)
    outs_n = len(parts) // 2
    flat = pl.pallas_call(
        functools.partial(block_kernel, len(parts), len(mids), places),
        out_shape=[jax.ShapeDtypeStruct((2 * half, width + tail), BF16)] * outs_n
        + [jax.ShapeDtypeStruct((m, units), BF16)] * 3
        + [jax.ShapeDtypeStruct((2, width), F32)],
        in_specs=[WHOLE] * (len(parts) + 3 * len(mids) + 5),
        out_specs=[WHOLE] * (outs_n + 4),
        compiler_params=PARAMS,
        cost_estimate=COST,
        name="block",
    )(*parts, *[value for mid in mids for value in mid], *weights, before)
    return flat[:outs_n], flat[outs_n : outs_n + 3], flat[-1]


def total_kernel(*refs):
    *part_refs, out_ref = refs
    out_ref[...] = sum(ref[...].astype(F32) for ref in part_refs)


def total_of(parts):
    return pl.pallas_call(
        total_kernel,
        out_shape=jax.ShapeDtypeStruct(parts[0].shape, F32),
        in_specs=[WHOLE] * len(parts),
        out_specs=WHOLE,
        compiler_params=PARAMS,
        cost_estimate=pl.CostEstimate(flops=1000000000, bytes_accessed=1, transcendentals=0),
        name="total_of",
    )(*parts)


def expand_kernel(dh_ref, far_ref, home_ref, small_ref, *refs):
    *others, out_ref = refs
    rows, width = dh_ref.shape
    dh = dh_ref[...] + far_ref[:, :width].astype(F32)
    out_ref[:, :width] = dot(home_ref[...], dh.astype(BF16)).astype(BF16)
    small = small_ref[...]
    for ref in others:
        small = small + ref[...]
    part = out_ref.shape[1] - width
    lines = lined(small, part)
    count = 2 * width // TAIL
    carried = far_ref[:, width:].astype(F32)
    carried = carried[:count] + carried[count : 2 * count]
    each = part // TAIL
    pieces = [
        jnp.concatenate([carried[q * each + k : q * each + k + 1] for k in range(each)], axis=1)
        for q in range(lines.shape[0])
    ]
    lines = (lines + stack(pieces)).astype(BF16)
    out_ref[:, width:] = jnp.concatenate([lines] * (out_ref.shape[0] // lines.shape[0]), axis=0)


def expand(dh, far, home, slots, *smalls):
    total = home.shape[0]
    width = dh.shape[1]
    return pl.pallas_call(
        expand_kernel,
        out_shape=jax.ShapeDtypeStruct((total, width + 2 * width // slots), BF16),
        in_specs=[WHOLE] * (3 + len(smalls)),
        out_specs=WHOLE,
        compiler_params=PARAMS,
        cost_estimate=COST,
        name="expand",
    )(dh, far, home, *smalls)


def finish_kernel(
    back_ref, picker_ref, tokens_ref, grad_ref, gain_ref, d_tokens_ref, d_gain_ref, d_router_ref
):
    total = back_ref.shape[0]
    width = tokens_ref.shape[1]
    experts = d_router_ref.shape[0]
    slots = total // experts
    half = slots // 2
    part = back_ref.shape[1] - width
    gain = gain_ref[...]
    tok = tokens_ref[...].astype(F32)
    inv_rms = lax.rsqrt(jnp.mean(tok * tok, axis=1, keepdims=True) + 1e-06)
    d_normed = dot(picker_ref[...], back_ref[:, :width], ((0,), (0,)))
    scaled = d_normed * gain
    inner = jnp.mean(scaled * tok, axis=1, keepdims=True)
    d_tokens_ref[...] = (
        grad_ref[...].astype(F32) + inv_rms * scaled - tok * (inv_rms * inv_rms * inv_rms * inner)
    ).astype(BF16)
    extra = back_ref[:, width:]
    slot = lax.broadcasted_iota(jnp.int32, (experts, total), 1)
    home = slots * lax.broadcasted_iota(jnp.int32, (experts, total), 0)
    place = lax.broadcasted_iota(jnp.int32, (slots, total), 1) % slots
    line = lax.broadcasted_iota(jnp.int32, (slots, total), 0)
    sums = dot((place == line).astype(BF16), extra)
    for q in range(half):
        at = slice(q * part, (q + 1) * part)
        d_router_ref[:, at] = dot((slot == home + q).astype(BF16), extra)
        d_gain_ref[:, at] = sums[half + q : half + q + 1, :] / gain[:, at]


def finish(back, picker, tokens, grad_out, norm_gain, experts):
    width = tokens.shape[1]
    return pl.pallas_call(
        finish_kernel,
        out_shape=(
            jax.ShapeDtypeStruct(tokens.shape, BF16),
            jax.ShapeDtypeStruct((1, width), F32),
            jax.ShapeDtypeStruct((experts, width), F32),
        ),
        in_specs=[WHOLE] * 5,
        out_specs=[WHOLE] * 3,
        compiler_params=PARAMS,
        cost_estimate=COST,
        name="finish",
    )(back, picker, tokens, grad_out, norm_gain)


def in_grads_kernel(n, *refs):
    w0_ref, w1_ref, pair_ref = refs[-3:]
    grads = refs[n:-3]
    units = w0_ref.shape[1]

    @pl.when(pl.program_id(0) == 0)
    def _():
        pair_ref[:, :units] = stack([ref[...] for ref in grads[0::2]])
        pair_ref[:, units:] = stack([ref[...] for ref in grads[1::2]])

    pair = dot(stack([ref[...] for ref in refs[:n]]), pair_ref[...], ((0,), (0,)))
    w0_ref[...] = pair[:, :units].astype(BF16)
    w1_ref[...] = pair[:, units:].astype(BF16)


def out_grad_kernel(n, *refs):
    wo_ref, act_ref = refs[-2:]

    @pl.when(pl.program_id(0) == 0)
    def _():
        act_ref[...] = stack([ref[...] for ref in refs[n:-2]]).T

    wo_ref[...] = dot(act_ref[...], stack([ref[...] for ref in refs[:n]])).astype(BF16)


def weight_grads(kernel, parts, which, factors, outs, scratch, tile=512):
    half, width = parts[0].shape[0] // 2, parts[0].shape[1]
    return pl.pallas_call(
        functools.partial(kernel, len(parts)),
        grid=(width // tile,),
        out_shape=[jax.ShapeDtypeStruct(shape, BF16) for shape in outs],
        in_specs=[pl.BlockSpec((half, tile), lambda i: (which, i))] * len(parts)
        + [pl.BlockSpec(value.shape, lambda i: (0, 0)) for value in factors],
        out_specs=[
            pl.BlockSpec((tile, shape[1]), lambda i: (i, 0))
            if shape[0] == width
            else pl.BlockSpec((shape[0], tile), lambda i: (0, i))
            for shape in outs
        ],
        scratch_shapes=[pltpu.VMEM(scratch, BF16)],
        compiler_params=PARAMS,
        cost_estimate=pl.CostEstimate(flops=2000000000, bytes_accessed=1, transcendentals=0),
        name="weight_grads",
    )(*parts, *factors)


def shift(value, axis, by):
    n = lax.axis_size(axis)
    return lax.ppermute(value, axis, [(i, (i + by) % n) for i in range(n)])


def exchange(value):
    return lax.all_to_all(value, "expert", split_axis=0, concat_axis=0, tiled=True)


def per_device(tokens, grad_out, norm_gain, router, w_in0, w_in1, w_out, slot_rows, slot_count):
    tok_dev, width = tokens.shape
    experts = router.shape[1]
    slots = slot_rows.shape[2]
    total = experts * slots
    w0, w1, wo = w_in0[0], w_in1[0], w_out[0]

    expert = lax.axis_index("expert")
    rrow = lax.dynamic_slice_in_dim(router.T, expert, 1, axis=0).astype(F32)
    names = slot_rows[0].T
    both = pick(tokens, grad_out, norm_gain.reshape(1, width), names, slot_count)
    picker = picker_of(names, slot_count, tok_dev)
    both = exchange(both.reshape(experts, 2 * slots, width)).reshape(2 * total, width)
    both, rrow, picker = lax.optimization_barrier((both, rrow, picker))
    first, second, place = pack(both, slots)
    weights = (w0, w1, wo, rrow)
    early = [shift(first, "dp", 1), shift(second, "dp", -1)]
    late = [shift(second, "dp", 1), shift(first, "dp", -1)]
    far = [shift(early[0], "dp", 1), shift(early[1], "dp", -1)]
    one = ((0, 0), (0, 1))
    mid_own, mid_early = hidden([[first, second], early], w0, w1)
    small = jnp.zeros((2, width), F32)
    (dh_own,), grads_own, small = block([first, second], [mid_own], weights, small, one)
    late, small = lax.optimization_barrier((late, small))
    (mid_late,) = hidden([late], w0, w1)
    place, small = lax.optimization_barrier((place, small))
    home = home_of(place, slots)
    dh_near, grads_near, small = block(
        early + late, [mid_early, mid_late], weights, small, ((0, 0), (1, 1), (0, 1), (1, 0))
    )
    far, small, home = lax.optimization_barrier((far, small, home))
    (mid_far,) = hidden([far], w0, w1)
    (dh_far,), grads_far, small = block(far, [mid_far], weights, small, one, TAIL)
    back_near = [shift(dh_near[0], "dp", -1), shift(dh_near[1], "dp", 1)]
    back_far = shift(dh_far, "dp", 2)
    smalls = [small, shift(small, "dp", 1), shift(small, "dp", -1)]

    parts = [first, second] + early + late + far
    grads = (*grads_own, *grads_near, *grads_far)
    rows, units = 4 * first.shape[0], w0.shape[1]
    grad_w0, grad_w1 = weight_grads(
        in_grads_kernel,
        parts,
        0,
        [part for k, part in enumerate(grads) if k % 3],
        [w0.shape, w1.shape],
        (rows, 2 * units),
    )
    (grad_wout,) = weight_grads(
        out_grad_kernel, parts, 1, list(grads[0::3]), [wo.shape], (units, rows)
    )
    back_far, grad_w0, grad_w1, grad_wout = lax.optimization_barrier(
        (back_far, grad_w0, grad_w1, grad_wout)
    )

    back = expand(total_of([dh_own, *back_near]), back_far, home, slots, *smalls)
    back = exchange(back.reshape(experts, slots, -1)).reshape(total, -1)
    d_tokens, d_gain, d_router = finish(
        back, picker, tokens, grad_out, norm_gain.reshape(1, width), experts
    )
    return (
        d_tokens,
        d_gain.reshape(width),
        d_router.T,
        grad_w0[None],
        grad_w1[None],
        grad_wout[None],
    )


def solution(mesh):
    in_specs = (
        P(("dp", "expert"), None),
        P(("dp", "expert"), None),
        P(),
        P(),
        P("expert", None, "dp"),
        P("expert", None, "dp"),
        P("expert", "dp", None),
        P(("dp", "expert"), None, None),
        P(("dp", "expert"), None),
    )
    out_specs = (
        P(("dp", "expert"), None),
        P(),
        P(),
        P("expert", None, "dp"),
        P("expert", None, "dp"),
        P("expert", "dp", None),
    )
    return jax.shard_map(
        per_device, mesh=mesh, in_specs=in_specs, out_specs=out_specs, check_vma=False
    )
```
